32 devices in a mesh: event: 2 (over y), dom: 4 (over z), sub: 2 (over x), lane: 2 (over core).
Axes of the slice: x: 2, y: 2, z: 4, core: 2. Of those that a mesh axis runs over, the one named last changes fastest.
Arguments:
- displacement: float32 [3, 65536], P(None, ('event', 'dom', 'sub', 'lane')), parts along dimension 1, may hold values from -6 to 6
- previous: float32 [3, 65536], P(None, ('event', 'dom', 'sub', 'lane')), parts along dimension 1, may hold values from -6 to 6
- traffic_load: float32 [2, 3, 65536], P(None, None, ('event', 'dom', 'sub', 'lane')), parts along dimension 2, may hold values from -6 to 6
- lumped_mass: float32 [32768], P(('dom', 'sub', 'lane')), may hold values from 1 to 4
- stiffness: float32 [32768], P(('dom', 'sub', 'lane')), may hold values from 0.2 to 2
- base_matrix: float32 [24, 24], replicated, as said below
- connectivity: int32 [8, 32768], P(None, ('dom', 'sub', 'lane')), may hold values from 0 to 6143, as said below
- live_elements: int32 [16], P(('dom', 'sub', 'lane')), may hold values from 512 to 2048, as said below
- sensor_nodes: int32 [2048], P(('dom', 'sub', 'lane')), may hold values from 0 to 2047
- sensor_weights: float32 [3, 4096], P(None, ('event', 'dom', 'sub', 'lane')), parts along dimension 1, may hold values from -6 to 6
Outputs:
- sensitivity: float32 [65536], P(('event', 'dom', 'sub', 'lane')), parts along dimension 0
- adjoint_start: float32 [3, 65536], P(None, ('event', 'dom', 'sub', 'lane')), parts along dimension 1
- sensor_response: float32 [3, 4096], P(None, ('event', 'dom', 'sub', 'lane')), parts along dimension 1
The draws below stay inside these ranges and needn't reach their ends.
There are 2 independent parts, one for each index of `event`. The reference program is written for one: setup_inputs(seed, part) draws one part's arguments, and reference() takes and returns one part's arrays. A program takes and returns all parts, laid end to end along the dimension named above; an argument that names none is the same for every part. Nothing has to cross between parts.
Inputs may be any that keep to these rules, and one draw needn't show every extreme that they name: `connectivity`: each slot's eight indices are b, b+1, b+4, b+5, b+2048, b+2048 + 1, b+2048 + 4, b+2048 + 5 for some b; window index w means node w of the node blocks of the device before, the device itself and the device after, laid end to end. `live_elements`: device 0 of every draw has all slots live. `base_matrix`: Symmetric.
All inputs are finite; a program needn't handle non-finite values.
Results may differ from the reference program's by a relative error of at most 0.00015.
Values sent between devices are 32-bit elements; how exact they have to be, the bound alone decides.
A program may use at most 64 MiB of HBM per device.

```python
import math
import jax
import jax.numpy as jnp
from jax import lax

NODE_DEV = 2048
ELEM_DEV = 2048
SENS_DEV = 128
NODES = 32768
DEVS = 16
ELEMENTS = 32768
SENSORS = 2048


def draw_base_matrix(key, part):
    key = jax.random.fold_in(key, 11)
    noise = jax.random.normal(key, (24, 24), jnp.float32) * 0.15
    return 0.5 * (noise + noise.T) + jnp.eye(24, dtype=jnp.float32)


def draw_connectivity(key, part):
    key = jax.random.fold_in(key, 12)
    corner = jax.random.randint(key, (1, ELEMENTS), 0, 2 * NODE_DEV - 5)
    corner = corner.at[0, 0].set(0).at[0, 1].set(2 * NODE_DEV - 6)
    offsets = jnp.array([0, 1, 4, 5, 0, 1, 4, 5], jnp.int32) + jnp.array([0, 0, 0, 0, 1, 1, 1, 1], jnp.int32) * NODE_DEV
    return (corner + offsets[:, None]).astype(jnp.int32)


def draw_live_elements(key, part):
    key = jax.random.fold_in(key, 13)
    counts = jax.random.randint(key, (DEVS,), ELEM_DEV // 4, ELEM_DEV + 1)
    return counts.at[0].set(ELEM_DEV).astype(jnp.int32)


def place_ends(values, stream_key, least, largest):
    place = [jax.random.randint(jax.random.fold_in(stream_key, axis), (), 0, length) for axis, length in enumerate(values.shape)]
    widest = values.shape.index(max(values.shape))
    next_to = place[:widest] + [(place[widest] + 1) % values.shape[widest]] + place[widest + 1:]
    return values.at[tuple(place)].set(least).at[tuple(next_to)].set(largest)


def block_levels(own_key, extent, pieces, least, largest):
    def one(position, blocks):
        heights = jax.random.uniform(jax.random.fold_in(jax.random.fold_in(own_key, 6), position), (blocks,), jnp.float32, least / len(pieces), largest / len(pieces))
        return jnp.repeat(jnp.exp(heights), extent[position] // blocks).reshape((-1,) + (1,) * (len(extent) - position - 1))

    loudness = one(*pieces[0])
    for cut in pieces[1:]:
        loudness = loudness * one(*cut)
    return loudness


def bell_draw(key, extent, deviation, reach, cuts=(), kind=jnp.bfloat16):
    values = jax.random.normal(key, extent, jnp.float32) * deviation
    if len(cuts) > 0:
        values = block_levels(key, extent, cuts, -0.22, 0.18) * values
    return jnp.clip(values, min=-reach, max=reach).astype(kind)


def setup_inputs(seed: int = 0, part: int = 0) -> dict:
    splits = jax.random.split(jax.random.key(seed), 11)
    part_keys = jax.random.split(jax.random.fold_in(splits[10], part), 11)
    displacement = bell_draw(part_keys[0], (3, NODES), 1.0, 6.0, ((1, 16),), jnp.float32)
    previous = bell_draw(part_keys[1], (3, NODES), 1.0, 6.0, ((1, 16),), jnp.float32)
    traffic_load = bell_draw(part_keys[2], (2, 3, NODES), 1.0, 6.0, ((2, 16),), jnp.float32)
    lumped_mass = jnp.clip(jnp.exp(math.log(4.0) - 1.3862944 * jax.random.uniform(splits[3], (NODES,), jnp.float32) ** block_levels(splits[3], (NODES,), ((0, 16),), -0.2, 0.2)), 1.0, 4.0)
    stiffness = jnp.clip(jnp.exp(math.log(2.0) - 2.3025851 * jax.random.uniform(splits[4], (ELEMENTS,), jnp.float32) ** block_levels(splits[4], (ELEMENTS,), ((0, 16),), -0.2, 0.2)), 0.2, 2.0)
    base_matrix = draw_base_matrix(jax.random.fold_in(splits[10], 71), part)
    connectivity = draw_connectivity(jax.random.fold_in(splits[10], 71), part)
    live_elements = draw_live_elements(jax.random.fold_in(splits[10], 71), part)
    sensor_nodes = place_ends(jax.random.randint(splits[8], (SENSORS,), 0, NODE_DEV), jax.random.fold_in(splits[8], 1), 0, NODE_DEV - 1).astype(jnp.int32)
    sensor_weights = bell_draw(part_keys[9], (3, SENSORS), 1.0, 6.0, ((1, 16),), jnp.float32)
    return dict(displacement=displacement, previous=previous, traffic_load=traffic_load, lumped_mass=lumped_mass, stiffness=stiffness, base_matrix=base_matrix, connectivity=connectivity, live_elements=live_elements, sensor_nodes=sensor_nodes, sensor_weights=sensor_weights)


def assemble(field, connectivity, scale, base_matrix):
    padded = jnp.pad(field, ((0, 0), (NODE_DEV, NODE_DEV)))
    owner = (jnp.arange(ELEMENTS) // ELEM_DEV).astype(jnp.int32)
    indices = connectivity + owner[None, :] * NODE_DEV
    local_vals = padded[:, indices].reshape(24, ELEMENTS)
    products = jnp.dot(base_matrix, local_vals, precision=lax.Precision.HIGHEST)
    forces = (products * scale[None, :]).reshape(3, 8, ELEMENTS)
    summed = jnp.zeros_like(padded).at[:, indices].add(forces)
    return summed[:, NODE_DEV:NODE_DEV + NODES], local_vals, products


def reference(displacement, previous, traffic_load, lumped_mass, stiffness, base_matrix, connectivity, live_elements, sensor_nodes, sensor_weights):
    slots = jnp.arange(ELEMENTS).astype(jnp.int32)
    live = ((slots % ELEM_DEV) < live_elements[slots // ELEM_DEV]).astype(jnp.float32)
    scale = stiffness * live
    force0, vals0, prod0 = assemble(displacement, connectivity, scale, base_matrix)
    step_one = 2.0 * displacement - previous + 0.1 * (traffic_load[0] - force0) / lumped_mass
    force1, vals1, prod1 = assemble(step_one, connectivity, scale, base_matrix)
    step_two = 2.0 * step_one - displacement + 0.1 * (traffic_load[1] - force1) / lumped_mass
    owners = (jnp.arange(SENSORS) // SENS_DEV).astype(jnp.int32)
    global_nodes = owners * NODE_DEV + sensor_nodes
    sensor_response = step_two[:, global_nodes]
    lam_two = jnp.zeros_like(displacement).at[:, global_nodes].add(sensor_weights)
    mu_two = 0.1 * lam_two / lumped_mass
    force_mu2, mvals2, mprod2 = assemble(mu_two, connectivity, scale, base_matrix)
    lam_one = 2.0 * lam_two - force_mu2
    mu_one = 0.1 * lam_one / lumped_mass
    force_mu1, mvals1, mprod1 = assemble(mu_one, connectivity, scale, base_matrix)
    adjoint_start = 2.0 * lam_one - force_mu1 - lam_two
    sensitivity = -live * (jnp.sum(mvals2 * prod1, axis=0) + jnp.sum(mvals1 * prod0, axis=0))
    return sensitivity, adjoint_start, sensor_response
```

```python
import functools

import jax
import jax.numpy as jnp
from jax import lax
from jax.experimental import pallas as pl
from jax.experimental.pallas import tpu as pltpu
from jax.sharding import PartitionSpec as P

F32 = jnp.float32
BF16 = jnp.bfloat16
I32 = jnp.int32
LANES = 128
OFFSETS = (0, 1, 4, 5)
CHAIN = ("dom", "sub", "lane")


def pieces(x):
    high = x.astype(BF16).astype(F32)
    return high, (x - high).astype(BF16).astype(F32)


def dot(a, b, rhs_dim=0):
    return lax.dot_general(
        a.astype(BF16), b.astype(BF16), (((1,), (rhs_dim,)), ((), ())), preferred_element_type=F32
    )


def iota(shape, dim):
    return lax.broadcasted_iota(I32, shape, dim)


def expanded_matrix(base):
    base_high, base_low = pieces(base)
    row = iota((64, 24), 0)
    comp = row & 3
    pick = jnp.where((iota((64, 24), 1) == comp * 8 + (row >> 3)) & (comp < 3), 1.0, 0.0)
    column = iota((24, 192), 1)
    group = column >> 5
    half = jnp.where(group < 4, group >> 1, group - 4)
    column_comp = column & 3
    node = half * 4 + ((column >> 3) & 3)
    spread = jnp.where((iota((24, 192), 0) == column_comp * 8 + node) & (column_comp < 3), 1.0, 0.0)
    high = dot(dot(pick, base_high), spread)
    low = dot(dot(pick, base_low), spread)
    out_row = iota((64, 192), 0)
    out_column = iota((64, 192), 1)
    same_field = ((out_row >> 2) & 1) == ((out_column >> 2) & 1)
    return jnp.where(same_field, jnp.where(out_column < 128, high, low), 0.0).astype(BF16)


def tiles_of(x):
    return jnp.concatenate(
        [x[:, s : s + LANES] for s in range(0, x.shape[1], LANES)], axis=0
    )


def kernel(
    count,
    disp_ref,
    prev_ref,
    load_ref,
    mass_ref,
    stiff_ref,
    base_ref,
    conn_ref,
    live_ref,
    snode_ref,
    sweight_ref,
    sens_out,
    adj_out,
    resp_out,
    w1,
    w2,
    xs,
    xf,
    p1,
    carry,
    w8,
    send1,
    recv1,
    send2,
    recv2,
):
    nodes = disp_ref.shape[1]
    slots = stiff_ref.shape[1]
    sensors = snode_ref.shape[1]
    n_tiles = nodes // LANES
    own = LANES + nodes
    cells = 2 * nodes + LANES
    lanes_n = lax.axis_size("lane")
    subs_n = lax.axis_size("sub")
    me = (lax.axis_index("dom") * subs_n + lax.axis_index("sub")) * lanes_n + lax.axis_index("lane")

    def there(step):
        other = me + step
        return {
            "dom": lax.div(other, lanes_n * subs_n),
            "sub": lax.rem(lax.div(other, lanes_n), subs_n),
            "lane": lax.rem(other, lanes_n),
        }

    def exists(step):
        return (me + step < count) if step > 0 else (me + step >= 0)

    steps = (1, -1, 2, -2)
    barrier = pltpu.get_barrier_semaphore()
    for step in steps:

        @pl.when(exists(step))
        def _(step=step):
            pl.semaphore_signal(
                barrier, inc=1, device_id=there(step), device_id_type=pl.DeviceIdType.MESH
            )

    sources = {1: (own, nodes), -1: (own, nodes), 2: (own + nodes - LANES, LANES), -2: (own, LANES)}
    targets = {1: LANES, -1: own + nodes, 2: 0, -2: own + 2 * nodes}

    def copy(w, send, recv, which):
        step = steps[which]
        start, width = sources[step]
        return pltpu.make_async_remote_copy(
            src_ref=w.at[:, pl.ds(start, width)],
            dst_ref=w.at[:, pl.ds(targets[step], width)],
            send_sem=send.at[which],
            recv_sem=recv.at[which],
            device_id=there(step),
            device_id_type=pl.DeviceIdType.MESH,
        )

    def start_all(w, send, recv):
        for which, step in enumerate(steps):

            @pl.when(exists(step))
            def _(which=which):
                copy(w, send, recv, which).start()

    def wait_arrivals(w, send, recv):
        for which, step in enumerate(steps):

            @pl.when(exists(-step))
            def _(which=which):
                copy(w, send, recv, which).wait_recv()

    def wait_sent(w, send, recv):
        for which, step in enumerate(steps):

            @pl.when(exists(step))
            def _(which=which):
                copy(w, send, recv, which).wait_send()

    for which, step in enumerate(steps):

        @pl.when(jnp.logical_not(exists(-step)))
        def _(step=step):
            width = sources[step][1]
            zero = jnp.zeros((8, width), F32)
            w1[:, pl.ds(targets[step], width)] = zero
            w2[:, pl.ds(targets[step], width)] = zero

    corner = conn_ref[0:1, :]
    corner_high = corner >> 7
    live = iota((1, slots), 1) < live_ref[0]
    scale_high, scale_low = pieces(jnp.where(live, stiff_ref[...], 0.0))
    rows = iota((8 * n_tiles, slots), 0)
    place = jnp.where((rows & 7) == 3, rows >> 3, jnp.where((rows & 7) == 7, (rows >> 3) + n_tiles, -1))
    on_row = place == corner_high
    weighted = jnp.concatenate(
        [
            jnp.where(on_row, scale_high, 0.0).astype(BF16),
            jnp.where(on_row, scale_low, 0.0).astype(BF16),
        ],
        axis=0,
    )
    low_hot = jnp.where(iota((LANES, slots), 0) == (corner & (LANES - 1)), 1.0, 0.0).astype(BF16)
    both = dot(weighted, low_hot, 1)
    factor = both[: 8 * n_tiles] + both[8 * n_tiles :]

    snode = snode_ref[...]
    sensor_high = snode >> 7
    sensor_hot = jnp.where(iota((LANES, sensors), 0) == (snode & (LANES - 1)), 1.0, 0.0).astype(BF16)
    w8[...] = jnp.zeros((8, sensors), F32)
    w8[4:7, :] = sweight_ref[...]
    weight_high, weight_low = pieces(w8[...])
    stacked = jnp.concatenate(
        [
            jnp.where(sensor_high == h, part, 0.0)
            for part in (weight_high, weight_low)
            for h in range(n_tiles)
        ],
        axis=0,
    )
    placed = dot(stacked, sensor_hot, 1)
    placed = placed[: 8 * n_tiles] + placed[8 * n_tiles :]
    lam2 = jnp.concatenate([placed[8 * h : 8 * h + 8] for h in range(n_tiles)], axis=1)
    factors = jnp.concatenate([factor[8 * h : 8 * h + 8] for h in range(n_tiles)], axis=1)

    inverse = 0.1 / mass_ref[...]
    mu2 = lam2 * inverse
    w1[:, pl.ds(own, nodes)] = mu2 + factors
    disp = disp_ref[...]
    w1[0:3, pl.ds(own, nodes)] = disp

    peers = sum(jnp.where(exists(step), 1, 0) for step in steps)
    pl.semaphore_wait(barrier, peers)

    start_all(w1, send1, recv1)

    lane = iota((8, LANES), 1)

    def shift_tiles(w, first, last, keep):
        def turned(t):
            x = w[:, t * LANES : (t + 1) * LANES]
            return [x] + [pltpu.roll(x, LANES - off, 1) for off in OFFSETS[1:]]

        now = turned(first)
        for t in range(first, last):
            after = turned(t + 1)
            full = jnp.concatenate(
                [now[0]]
                + [
                    jnp.where(lane < LANES - off, now[i], after[i])
                    for i, off in enumerate(OFFSETS)
                    if i > 0
                ],
                axis=0,
            )
            if keep:
                xf[:, t * LANES : (t + 1) * LANES] = full
            high = full.astype(BF16)
            xs[0:32, t * LANES : (t + 1) * LANES] = high
            xs[32:64, t * LANES : (t + 1) * LANES] = (full - high.astype(F32)).astype(BF16)
            now = after

    def operand(start, width):
        return jnp.concatenate(
            [
                xs[:, start : start + width],
                xs[:, start + nodes : start + nodes + width],
                xs[0:32, start : start + width],
                xs[0:32, start + nodes : start + nodes + width],
            ],
            axis=0,
        )

    matrix = expanded_matrix(base_ref[...])
    carry[...] = 2.0 * mu2
    carry[0:3, :] = 2.0 * disp - prev_ref[...] + load_ref[0] * inverse
    first_own = own // LANES
    last_tile = own // LANES + 2 * n_tiles
    shift_tiles(w1, first_own, first_own + n_tiles - 1, False)

    wait_arrivals(w1, send1, recv1)
    shift_tiles(w1, 0, first_own, False)
    shift_tiles(w1, first_own + n_tiles - 1, last_tile, False)

    total = w1[3:4, nodes : nodes + cells] + w1[7:8, 0:cells]
    width = nodes + LANES

    def spread_sum(half0, half1):
        near, far = total[:, nodes:], total[:, :width]
        out = None
        for i, off in enumerate(OFFSETS):
            part = half0[8 * i : 8 * i + 8] * near + half1[8 * i : 8 * i + 8] * far
            part = pltpu.roll(part, off, 1) if off else part
            out = part if out is None else out + part
        return out[:, LANES:]

    p1[...] = dot(matrix, operand(0, cells))
    force = spread_sum(p1[0:32, nodes:], p1[32:64, :width])
    stepped = carry[...] - inverse * force
    w2[:, pl.ds(own, nodes)] = pltpu.roll(stepped, 4, 0)
    start_all(w2, send2, recv2)

    adjoint = pltpu.roll(3.0 * lam2 - 2.0 * force, 4, 0)
    carry[...] = 2.0 * stepped
    carry[0:3, :] = 2.0 * stepped[0:3] - disp + load_ref[1] * inverse

    shift_tiles(w2, first_own, first_own + n_tiles - 1, True)
    wait_arrivals(w2, send2, recv2)
    shift_tiles(w2, 0, first_own, True)
    shift_tiles(w2, first_own + n_tiles - 1, last_tile, True)

    force2 = spread_sum(
        dot(matrix[0:32], operand(nodes, width)), dot(matrix[32:64], operand(0, width))
    )
    adj_out[...] = (adjoint - force2)[0:3]
    final = carry[...] - inverse * pltpu.roll(force2, 4, 0)

    picked = dot(
        jnp.concatenate(pieces(tiles_of(final)), axis=1),
        jnp.concatenate([sensor_hot, sensor_hot], axis=0),
    )
    response = jnp.zeros((8, sensors), F32)
    for h in range(n_tiles):
        response = response + jnp.where(sensor_high == h, picked[8 * h : 8 * h + 8], 0.0)
    resp_out[...] = response[0:3]

    energy = None
    for k in range(8):
        shift = LANES + (k // 4) * nodes
        part = (
            xf[8 * (k % 4) : 8 * (k % 4) + 8, shift : shift + 2 * nodes]
            * p1[8 * k : 8 * k + 8, LANES:cells]
        )
        energy = part if energy is None else energy + part
    table = jnp.concatenate(pieces(tiles_of(energy)), axis=1)
    found = dot(table, jnp.concatenate([low_hot, low_hot], axis=0))
    gathered = jnp.zeros((8, slots), F32)
    for h in range(2 * n_tiles):
        gathered = gathered + jnp.where(corner_high == h, found[8 * h : 8 * h + 8], 0.0)
    gathered = jnp.sum(gathered, axis=0, keepdims=True)
    sens_out[...] = jnp.where(live, -gathered, 0.0)

    wait_sent(w1, send1, recv1)
    wait_sent(w2, send2, recv2)


def per_device(
    displacement,
    previous,
    traffic_load,
    lumped_mass,
    stiffness,
    base_matrix,
    connectivity,
    live_elements,
    sensor_nodes,
    sensor_weights,
):
    nodes = displacement.shape[1]
    slots = connectivity.shape[1]
    sensors = sensor_nodes.shape[0]
    count = lax.axis_size(CHAIN)
    window = 3 * nodes + 2 * LANES
    vmem = pl.BlockSpec(memory_space=pltpu.VMEM)
    smem = pl.BlockSpec(memory_space=pltpu.SMEM)
    sensitivity, adjoint_start, sensor_response = pl.pallas_call(
        functools.partial(kernel, count),
        out_shape=(
            jax.ShapeDtypeStruct((1, slots), F32),
            jax.ShapeDtypeStruct((3, nodes), F32),
            jax.ShapeDtypeStruct((3, sensors), F32),
        ),
        in_specs=[vmem] * 7 + [smem] + [vmem] * 2,
        out_specs=(vmem, vmem, vmem),
        scratch_shapes=[
            pltpu.VMEM((8, window), F32),
            pltpu.VMEM((8, window), F32),
            pltpu.VMEM((64, window), BF16),
            pltpu.VMEM((32, window), F32),
            pltpu.VMEM((64, 2 * nodes + LANES), F32),
            pltpu.VMEM((8, nodes), F32),
            pltpu.VMEM((8, sensors), F32),
            pltpu.SemaphoreType.DMA((4,)),
            pltpu.SemaphoreType.DMA((4,)),
            pltpu.SemaphoreType.DMA((4,)),
            pltpu.SemaphoreType.DMA((4,)),
        ],
        compiler_params=pltpu.CompilerParams(
            collective_id=0, has_side_effects=True, vmem_limit_bytes=32 * 1024 * 1024
        ),
    )(
        displacement,
        previous,
        traffic_load,
        lumped_mass.reshape(1, nodes),
        stiffness.reshape(1, slots),
        base_matrix,
        connectivity,
        live_elements,
        sensor_nodes.reshape(1, sensors),
        sensor_weights,
    )
    return sensitivity.reshape(slots), adjoint_start, sensor_response


def solution(mesh):
    in_specs = (
        P(None, ("event", "dom", "sub", "lane")),
        P(None, ("event", "dom", "sub", "lane")),
        P(None, None, ("event", "dom", "sub", "lane")),
        P(("dom", "sub", "lane")),
        P(("dom", "sub", "lane")),
        P(),
        P(None, ("dom", "sub", "lane")),
        P(("dom", "sub", "lane")),
        P(("dom", "sub", "lane")),
        P(None, ("event", "dom", "sub", "lane")),
    )
    out_specs = (
        P(("event", "dom", "sub", "lane")),
        P(None, ("event", "dom", "sub", "lane")),
        P(None, ("event", "dom", "sub", "lane")),
    )
    return jax.shard_map(
        per_device, mesh=mesh, in_specs=in_specs, out_specs=out_specs, check_vma=False
    )
```

```python
import functools

import jax
import jax.numpy as jnp
from jax import lax
from jax.experimental import pallas as pl
from jax.experimental.pallas import tpu as pltpu
from jax.sharding import PartitionSpec as P

F32 = jnp.float32
BF16 = jnp.bfloat16
I32 = jnp.int32
LANES = 128
OFFSETS = (0, 1, 4, 5)
CHAIN = ("dom", "sub", "lane")


def pieces(x):
    high = x.astype(BF16).astype(F32)
    return high, (x - high).astype(BF16).astype(F32)


def dot(a, b, rhs_dim=0):
    return lax.dot_general(
        a.astype(BF16), b.astype(BF16), (((1,), (rhs_dim,)), ((), ())), preferred_element_type=F32
    )


def iota(shape, dim):
    return lax.broadcasted_iota(I32, shape, dim)


def expanded_matrix(base):
    base_high, base_low = pieces(base)
    row = iota((64, 24), 0)
    comp = row & 3
    pick = jnp.where((iota((64, 24), 1) == comp * 8 + (row >> 3)) & (comp < 3), 1.0, 0.0)
    column = iota((24, 192), 1)
    group = column >> 5
    half = jnp.where(group < 4, group >> 1, group - 4)
    column_comp = column & 3
    node = half * 4 + ((column >> 3) & 3)
    spread = jnp.where((iota((24, 192), 0) == column_comp * 8 + node) & (column_comp < 3), 1.0, 0.0)
    high = dot(dot(pick, base_high), spread)
    low = dot(dot(pick, base_low), spread)
    out_row = iota((64, 192), 0)
    out_column = iota((64, 192), 1)
    same_field = ((out_row >> 2) & 1) == ((out_column >> 2) & 1)
    return jnp.where(same_field, jnp.where(out_column < 128, high, low), 0.0).astype(BF16)


def tiles_of(x):
    return jnp.concatenate(
        [x[:, s : s + LANES] for s in range(0, x.shape[1], LANES)], axis=0
    )


def row_sums(blocks):
    sub = iota((8, LANES), 0)
    step = 4
    while step:
        keep = (sub & step) == 0
        blocks = [
            jnp.where(keep, a, b)
            + jnp.where(keep, pltpu.roll(a, 8 - step, 0), pltpu.roll(b, step, 0))
            for a, b in zip(blocks[:step], blocks[step:])
        ]
        step //= 2
    return blocks[0]


def kernel(
    count,
    disp_hbm,
    prev_hbm,
    load_hbm,
    mass_hbm,
    stiff_hbm,
    base_hbm,
    conn_hbm,
    live_hbm,
    snode_hbm,
    sweight_hbm,
    sens_out,
    adj_out,
    resp_out,
    disp_ref,
    prev_ref,
    load_ref,
    mass_ref,
    stiff_ref,
    base_ref,
    conn_ref,
    live_ref,
    snode_ref,
    sweight_ref,
    loaded,
    w1,
    w2,
    st,
    xs,
    xf,
    p1,
    carry,
    w8,
    send1,
    recv1,
    send2,
    recv2,
    send3,
    recv3,
):
    nodes = disp_ref.shape[1]
    slots = stiff_ref.shape[1]
    sensors = snode_ref.shape[1]
    n_tiles = nodes // LANES
    own = LANES + nodes
    cells = 2 * nodes + LANES
    lanes_n = lax.axis_size("lane")
    subs_n = lax.axis_size("sub")
    me = (lax.axis_index("dom") * subs_n + lax.axis_index("sub")) * lanes_n + lax.axis_index("lane")

    def there(step):
        other = me + step
        return {
            "dom": lax.div(other, lanes_n * subs_n),
            "sub": lax.rem(lax.div(other, lanes_n), subs_n),
            "lane": lax.rem(other, lanes_n),
        }

    def exists(step):
        return (me + step < count) if step > 0 else (me + step >= 0)

    steps = (1, -1, 2, -2)
    barrier = pltpu.get_barrier_semaphore()
    for step in steps:

        @pl.when(exists(step))
        def _(step=step):
            pl.semaphore_signal(
                barrier, inc=1, device_id=there(step), device_id_type=pl.DeviceIdType.MESH
            )

    loads = {
        i: pltpu.make_async_copy(source, target, loaded.at[i])
        for i, (source, target) in enumerate(
            (
                (snode_hbm, snode_ref),
                (sweight_hbm, sweight_ref),
                (mass_hbm, mass_ref),
                (disp_hbm, disp_ref),
                (conn_hbm, conn_ref),
                (stiff_hbm, stiff_ref),
                (live_hbm, live_ref),
                (base_hbm, base_ref),
                (prev_hbm, prev_ref),
                (load_hbm, load_ref),
            )
        )
    }
    for load in loads.values():
        load.start()

    sources = {1: (own, nodes), -1: (own, nodes), 2: (own + nodes - LANES, LANES), -2: (own, LANES)}
    targets = {1: LANES, -1: own + nodes, 2: 0, -2: own + 2 * nodes}

    def copy(w, send, recv, which):
        step = steps[which]
        start, width = sources[step]
        return pltpu.make_async_remote_copy(
            src_ref=w.at[:, pl.ds(start, width)],
            dst_ref=w.at[:, pl.ds(targets[step], width)],
            send_sem=send.at[which],
            recv_sem=recv.at[which],
            device_id=there(step),
            device_id_type=pl.DeviceIdType.MESH,
        )

    def start_all(w, send, recv):
        for which, step in enumerate(steps):

            @pl.when(exists(step))
            def _(which=which):
                copy(w, send, recv, which).start()

    def wait_arrivals(w, send, recv):
        for which, step in enumerate(steps):

            @pl.when(exists(-step))
            def _(which=which):
                copy(w, send, recv, which).wait_recv()

    def wait_sent(w, send, recv):
        for which, step in enumerate(steps):

            @pl.when(exists(step))
            def _(which=which):
                copy(w, send, recv, which).wait_send()

    for which, step in enumerate(steps):

        @pl.when(jnp.logical_not(exists(-step)))
        def _(step=step):
            width = sources[step][1]
            zero = jnp.zeros((8, width), F32)
            w1[:, pl.ds(targets[step], width)] = zero
            w2[:, pl.ds(targets[step], width)] = zero

    def copy_factors(which):
        return pltpu.make_async_remote_copy(
            src_ref=st.at[1],
            dst_ref=st.at[0 if which == 0 else 2],
            send_sem=send3.at[which],
            recv_sem=recv3.at[which],
            device_id=there(steps[which]),
            device_id_type=pl.DeviceIdType.MESH,
        )

    for which in range(2):

        @pl.when(jnp.logical_not(exists(-steps[which])))
        def _(which=which):
            st[0 if which == 0 else 2] = jnp.zeros((2 * n_tiles, LANES), F32)

    w8[...] = jnp.zeros((8, sensors), F32)
    for i in range(4):
        loads[i].wait()
    snode = snode_ref[...]
    sensor_high = snode >> 7
    sensor_hot = jnp.where(iota((LANES, sensors), 0) == (snode & (LANES - 1)), 1.0, 0.0).astype(BF16)
    w8[4:7, :] = sweight_ref[...]
    weight_high, weight_low = pieces(w8[...])
    stacked = jnp.concatenate(
        [
            jnp.where(sensor_high == h, part, 0.0)
            for part in (weight_high, weight_low)
            for h in range(n_tiles)
        ],
        axis=0,
    )
    placed = dot(stacked, sensor_hot, 1)
    placed = placed[: 8 * n_tiles] + placed[8 * n_tiles :]
    lam2 = jnp.concatenate([placed[8 * h : 8 * h + 8] for h in range(n_tiles)], axis=1)

    inverse = 0.1 / mass_ref[...]
    mu2 = lam2 * inverse
    w1[:, pl.ds(own, nodes)] = mu2
    disp = disp_ref[...]
    w1[0:3, pl.ds(own, nodes)] = disp

    peers = sum(jnp.where(exists(step), 1, 0) for step in steps)
    pl.semaphore_wait(barrier, peers)
    start_all(w1, send1, recv1)

    for i in range(4, 7):
        loads[i].wait()
    corner = conn_ref[0:1, :]
    corner_high = corner >> 7
    live = iota((1, slots), 1) < live_ref[0]
    scale_high, scale_low = pieces(jnp.where(live, stiff_ref[...], 0.0))
    on_row = iota((2 * n_tiles, slots), 0) == corner_high
    weighted = jnp.concatenate(
        [
            jnp.where(on_row, scale_high, 0.0).astype(BF16),
            jnp.where(on_row, scale_low, 0.0).astype(BF16),
        ],
        axis=0,
    )
    low_hot = jnp.where(iota((LANES, slots), 0) == (corner & (LANES - 1)), 1.0, 0.0).astype(BF16)
    both = dot(weighted, low_hot, 1)
    st[1] = both[: 2 * n_tiles] + both[2 * n_tiles :]
    for which in range(2):

        @pl.when(exists(steps[which]))
        def _(which=which):
            copy_factors(which).start()

    for i in range(7, 10):
        loads[i].wait()

    lane = iota((8, LANES), 1)

    def shift_tiles(w, first, last, keep):
        def turned(t):
            x = w[:, t * LANES : (t + 1) * LANES]
            return [x] + [pltpu.roll(x, LANES - off, 1) for off in OFFSETS[1:]]

        now = turned(first)
        for t in range(first, last):
            after = turned(t + 1)
            full = jnp.concatenate(
                [now[0]]
                + [
                    jnp.where(lane < LANES - off, now[i], after[i])
                    for i, off in enumerate(OFFSETS)
                    if i > 0
                ],
                axis=0,
            )
            if keep:
                xf[:, t * LANES : (t + 1) * LANES] = full
            high = full.astype(BF16)
            xs[0:32, t * LANES : (t + 1) * LANES] = high
            xs[32:64, t * LANES : (t + 1) * LANES] = (full - high.astype(F32)).astype(BF16)
            now = after

    def operand(start, width):
        return jnp.concatenate(
            [
                xs[:, start : start + width],
                xs[:, start + nodes : start + nodes + width],
                xs[0:32, start : start + width],
                xs[0:32, start + nodes : start + nodes + width],
            ],
            axis=0,
        )

    matrix = expanded_matrix(base_ref[...])
    carry[...] = 2.0 * mu2
    carry[0:3, :] = 2.0 * disp - prev_ref[...] + load_ref[:, 0, :] * inverse
    first_own = own // LANES
    last_tile = own // LANES + 2 * n_tiles
    shift_tiles(w1, first_own, first_own + n_tiles - 1, False)

    wait_arrivals(w1, send1, recv1)
    shift_tiles(w1, 0, first_own, False)
    shift_tiles(w1, first_own + n_tiles - 1, last_tile, False)

    for which in range(2):

        @pl.when(exists(-steps[which]))
        def _(which=which):
            copy_factors(which).wait_recv()

    def lower(tile):
        return st[tile // n_tiles, tile % n_tiles : tile % n_tiles + 1, :]

    def upper(tile):
        row = n_tiles + tile % n_tiles
        return st[tile // n_tiles, row : row + 1, :]

    totals = [lower(n_tiles - 1)] + [
        lower(t + n_tiles) + upper(t) for t in range(2 * n_tiles)
    ]
    total = jnp.concatenate([jnp.broadcast_to(x, (8, LANES)) for x in totals], axis=1)
    width = nodes + LANES

    def spread_sum(half0, half1):
        near, far = total[:, nodes:], total[:, :width]
        out = None
        for i, off in enumerate(OFFSETS):
            part = half0[8 * i : 8 * i + 8] * near + half1[8 * i : 8 * i + 8] * far
            part = pltpu.roll(part, off, 1) if off else part
            out = part if out is None else out + part
        return out[:, LANES:]

    p1[...] = dot(matrix, operand(0, cells))
    force = spread_sum(p1[0:32, nodes:], p1[32:64, :width])
    stepped = carry[...] - inverse * force
    w2[:, pl.ds(own, nodes)] = pltpu.roll(stepped, 4, 0)
    start_all(w2, send2, recv2)

    adjoint = pltpu.roll(3.0 * lam2 - 2.0 * force, 4, 0)
    carry[...] = 2.0 * stepped
    carry[0:3, :] = 2.0 * stepped[0:3] - disp + load_ref[:, 1, :] * inverse

    shift_tiles(w2, first_own, first_own + n_tiles - 1, True)
    wait_arrivals(w2, send2, recv2)
    shift_tiles(w2, 0, first_own, True)
    shift_tiles(w2, first_own + n_tiles - 1, last_tile, True)

    force2 = spread_sum(
        dot(matrix[0:32], operand(nodes, width)), dot(matrix[32:64], operand(0, width))
    )
    adj_out[...] = (adjoint - force2)[0:3]
    final = carry[...] - inverse * pltpu.roll(force2, 4, 0)

    picked = dot(
        jnp.concatenate(pieces(tiles_of(final)), axis=1),
        jnp.concatenate([sensor_hot, sensor_hot], axis=0),
    )
    response = jnp.zeros((8, sensors), F32)
    for h in range(n_tiles):
        response = response + jnp.where(sensor_high == h, picked[8 * h : 8 * h + 8], 0.0)
    resp_out[...] = response[0:3]

    energy = None
    for k in range(8):
        shift = LANES + (k // 4) * nodes
        part = (
            xf[8 * (k % 4) : 8 * (k % 4) + 8, shift : shift + 2 * nodes]
            * p1[8 * k : 8 * k + 8, LANES:cells]
        )
        energy = part if energy is None else energy + part
    tiles = [energy[:, t * LANES : (t + 1) * LANES] for t in range(2 * n_tiles)]
    sums = jnp.concatenate(
        [row_sums(tiles[t : t + 8]) for t in range(0, 2 * n_tiles, 8)], axis=0
    )
    table = jnp.concatenate(pieces(sums), axis=1)
    found = dot(table, jnp.concatenate([low_hot, low_hot], axis=0))
    gathered = jnp.sum(jnp.where(on_row, found, 0.0), axis=0, keepdims=True)
    sens_out[...] = jnp.where(live, -gathered, 0.0)

    for which in range(2):

        @pl.when(exists(steps[which]))
        def _(which=which):
            copy_factors(which).wait_send()

    wait_sent(w1, send1, recv1)
    wait_sent(w2, send2, recv2)


def store_kernel(sens, adj, resp, sens_out, adj_out, resp_out, sem):
    copies = [
        pltpu.make_async_copy(source, target, sem.at[i])
        for i, (source, target) in enumerate(((sens, sens_out), (adj, adj_out), (resp, resp_out)))
    ]
    for one in copies:
        one.start()
    for one in copies:
        one.wait()


def per_device(
    displacement,
    previous,
    traffic_load,
    lumped_mass,
    stiffness,
    base_matrix,
    connectivity,
    live_elements,
    sensor_nodes,
    sensor_weights,
):
    nodes = displacement.shape[1]
    slots = connectivity.shape[1]
    sensors = sensor_nodes.shape[0]
    count = lax.axis_size(CHAIN)
    window = 3 * nodes + 2 * LANES
    vmem = pl.BlockSpec(memory_space=pltpu.VMEM)
    hbm = pl.BlockSpec(memory_space=pltpu.HBM)
    operands = (
        displacement,
        previous,
        jnp.transpose(traffic_load, (1, 0, 2)),
        lumped_mass.reshape(1, nodes),
        stiffness.reshape(1, slots),
        base_matrix,
        connectivity,
        live_elements,
        sensor_nodes.reshape(1, sensors),
        sensor_weights,
    )
    results = pl.pallas_call(
        functools.partial(kernel, count),
        out_shape=(
            pltpu.VMEM((1, slots), F32),
            pltpu.VMEM((3, nodes), F32),
            pltpu.VMEM((3, sensors), F32),
        ),
        in_specs=[hbm] * len(operands),
        out_specs=(vmem, vmem, vmem),
        scratch_shapes=[
            (pltpu.SMEM if x is live_elements else pltpu.VMEM)(x.shape, x.dtype) for x in operands
        ]
        + [
            pltpu.SemaphoreType.DMA((len(operands),)),
            pltpu.VMEM((8, window), F32),
            pltpu.VMEM((8, window), F32),
            pltpu.VMEM((3, 2 * nodes // LANES, LANES), F32),
            pltpu.VMEM((64, window), BF16),
            pltpu.VMEM((32, window), F32),
            pltpu.VMEM((64, 2 * nodes + LANES), F32),
            pltpu.VMEM((8, nodes), F32),
            pltpu.VMEM((8, sensors), F32),
            pltpu.SemaphoreType.DMA((4,)),
            pltpu.SemaphoreType.DMA((4,)),
            pltpu.SemaphoreType.DMA((4,)),
            pltpu.SemaphoreType.DMA((4,)),
            pltpu.SemaphoreType.DMA((2,)),
            pltpu.SemaphoreType.DMA((2,)),
        ],
        compiler_params=pltpu.CompilerParams(
            collective_id=0, has_side_effects=True, vmem_limit_bytes=60 * 1024 * 1024
        ),
    )(*operands)
    sensitivity, adjoint_start, sensor_response = pl.pallas_call(
        store_kernel,
        out_shape=tuple(jax.ShapeDtypeStruct(x.shape, x.dtype) for x in results),
        in_specs=[vmem] * 3,
        out_specs=(hbm,) * 3,
        scratch_shapes=[pltpu.SemaphoreType.DMA((3,))],
    )(*results)
    return sensitivity.reshape(slots), adjoint_start, sensor_response


def solution(mesh):
    in_specs = (
        P(None, ("event", "dom", "sub", "lane")),
        P(None, ("event", "dom", "sub", "lane")),
        P(None, None, ("event", "dom", "sub", "lane")),
        P(("dom", "sub", "lane")),
        P(("dom", "sub", "lane")),
        P(),
        P(None, ("dom", "sub", "lane")),
        P(("dom", "sub", "lane")),
        P(("dom", "sub", "lane")),
        P(None, ("event", "dom", "sub", "lane")),
    )
    out_specs = (
        P(("event", "dom", "sub", "lane")),
        P(None, ("event", "dom", "sub", "lane")),
        P(None, ("event", "dom", "sub", "lane")),
    )
    return jax.shard_map(
        per_device, mesh=mesh, in_specs=in_specs, out_specs=out_specs, check_vma=False
    )
```

```python
import functools

import jax
import jax.numpy as jnp
from jax import lax
from jax.experimental import pallas as pl
from jax.experimental.pallas import tpu as pltpu
from jax.sharding import PartitionSpec as P

F32 = jnp.float32
BF16 = jnp.bfloat16
I32 = jnp.int32
LANES = 128
OFFSETS = (0, 1, 4, 5)
CHAIN = ("dom", "sub", "lane")


def pieces(x):
    high = x.astype(BF16).astype(F32)
    return high, (x - high).astype(BF16).astype(F32)


def dot(a, b, rhs_dim=0):
    return lax.dot_general(
        a.astype(BF16), b.astype(BF16), (((1,), (rhs_dim,)), ((), ())), preferred_element_type=F32
    )


def iota(shape, dim):
    return lax.broadcasted_iota(I32, shape, dim)


def expanded_matrix(base):
    base_high, base_low = pieces(base)
    row = iota((64, 24), 0)
    comp = row & 3
    pick = jnp.where((iota((64, 24), 1) == comp * 8 + (row >> 3)) & (comp < 3), 1.0, 0.0)
    column = iota((24, 192), 1)
    group = column >> 5
    half = jnp.where(group < 4, group >> 1, group - 4)
    column_comp = column & 3
    node = half * 4 + ((column >> 3) & 3)
    spread = jnp.where((iota((24, 192), 0) == column_comp * 8 + node) & (column_comp < 3), 1.0, 0.0)
    high = dot(dot(pick, base_high), spread)
    low = dot(dot(pick, base_low), spread)
    out_row = iota((64, 192), 0)
    out_column = iota((64, 192), 1)
    same_field = ((out_row >> 2) & 1) == ((out_column >> 2) & 1)
    return jnp.where(same_field, jnp.where(out_column < 128, high, low), 0.0).astype(BF16)


def tiles_of(x):
    return jnp.concatenate(
        [x[:, s : s + LANES] for s in range(0, x.shape[1], LANES)], axis=0
    )


def row_sums(blocks):
    sub = iota((8, LANES), 0)
    step = 4
    while step:
        keep = (sub & step) == 0
        blocks = [
            jnp.where(keep, a, b)
            + jnp.where(keep, pltpu.roll(a, 8 - step, 0), pltpu.roll(b, step, 0))
            for a, b in zip(blocks[:step], blocks[step:])
        ]
        step //= 2
    return blocks[0]


def kernel(
    count,
    disp_hbm,
    prev_hbm,
    load_hbm,
    mass_hbm,
    stiff_hbm,
    base_hbm,
    conn_hbm,
    live_hbm,
    snode_hbm,
    sweight_hbm,
    sens_out,
    adj_out,
    resp_out,
    disp_ref,
    prev_ref,
    load_ref,
    mass_ref,
    stiff_ref,
    base_ref,
    conn_ref,
    live_ref,
    snode_ref,
    sweight_ref,
    loaded,
    w1,
    w2,
    st,
    xs,
    xf,
    p1,
    carry,
    w8,
    send1,
    recv1,
    send2,
    recv2,
    send3,
    recv3,
):
    nodes = disp_ref.shape[1]
    slots = stiff_ref.shape[1]
    sensors = snode_ref.shape[1]
    n_tiles = nodes // LANES
    own = LANES + nodes
    cells = 2 * nodes + LANES
    lanes_n = lax.axis_size("lane")
    subs_n = lax.axis_size("sub")
    me = (lax.axis_index("dom") * subs_n + lax.axis_index("sub")) * lanes_n + lax.axis_index("lane")

    def there(step):
        other = me + step
        return {
            "dom": lax.div(other, lanes_n * subs_n),
            "sub": lax.rem(lax.div(other, lanes_n), subs_n),
            "lane": lax.rem(other, lanes_n),
        }

    def exists(step):
        return (me + step < count) if step > 0 else (me + step >= 0)

    steps = (1, -1, 2, -2)
    barrier = pltpu.get_barrier_semaphore()
    for step in steps:

        @pl.when(exists(step))
        def _(step=step):
            pl.semaphore_signal(
                barrier, inc=1, device_id=there(step), device_id_type=pl.DeviceIdType.MESH
            )

    loads = {
        i: pltpu.make_async_copy(source, target, loaded.at[i])
        for i, (source, target) in enumerate(
            (
                (snode_hbm, snode_ref),
                (sweight_hbm, sweight_ref),
                (mass_hbm, mass_ref),
                (disp_hbm, disp_ref),
                (conn_hbm, conn_ref),
                (stiff_hbm, stiff_ref),
                (live_hbm, live_ref),
                (base_hbm, base_ref),
                (prev_hbm, prev_ref),
                (load_hbm, load_ref),
            )
        )
    }
    for load in loads.values():
        load.start()

    sources = {1: (own, nodes), -1: (own, nodes), 2: (own + nodes - LANES, LANES), -2: (own, LANES)}
    targets = {1: LANES, -1: own + nodes, 2: 0, -2: own + 2 * nodes}

    def copy(w, send, recv, which):
        step = steps[which]
        start, width = sources[step]
        return pltpu.make_async_remote_copy(
            src_ref=w.at[:, pl.ds(start, width)],
            dst_ref=w.at[:, pl.ds(targets[step], width)],
            send_sem=send.at[which],
            recv_sem=recv.at[which],
            device_id=there(step),
            device_id_type=pl.DeviceIdType.MESH,
        )

    def start_all(w, send, recv):
        for which, step in enumerate(steps):

            @pl.when(exists(step))
            def _(which=which):
                copy(w, send, recv, which).start()

    def wait_arrivals(w, send, recv):
        for which, step in enumerate(steps):

            @pl.when(exists(-step))
            def _(which=which):
                copy(w, send, recv, which).wait_recv()

    def wait_sent(w, send, recv):
        for which, step in enumerate(steps):

            @pl.when(exists(step))
            def _(which=which):
                copy(w, send, recv, which).wait_send()

    for which, step in enumerate(steps):

        @pl.when(jnp.logical_not(exists(-step)))
        def _(step=step):
            width = sources[step][1]
            zero = jnp.zeros((8, width), F32)
            w1[:, pl.ds(targets[step], width)] = zero
            w2[:, pl.ds(targets[step], width)] = zero

    def copy_factors(which):
        return pltpu.make_async_remote_copy(
            src_ref=st.at[1],
            dst_ref=st.at[0 if which == 0 else 2],
            send_sem=send3.at[which],
            recv_sem=recv3.at[which],
            device_id=there(steps[which]),
            device_id_type=pl.DeviceIdType.MESH,
        )

    for which in range(2):

        @pl.when(jnp.logical_not(exists(-steps[which])))
        def _(which=which):
            st[0 if which == 0 else 2] = jnp.zeros((2 * n_tiles, LANES), F32)

    w8[...] = jnp.zeros((8, sensors), F32)
    for i in range(4):
        loads[i].wait()
    snode = snode_ref[...]
    sensor_high = snode >> 7
    sensor_hot = jnp.where(iota((LANES, sensors), 0) == (snode & (LANES - 1)), 1.0, 0.0).astype(BF16)
    w8[4:7, :] = sweight_ref[...]
    weight_high, weight_low = pieces(w8[...])
    stacked = jnp.concatenate(
        [
            jnp.where(sensor_high == h, part, 0.0)
            for part in (weight_high, weight_low)
            for h in range(n_tiles)
        ],
        axis=0,
    )
    placed = dot(stacked, sensor_hot, 1)
    placed = placed[: 8 * n_tiles] + placed[8 * n_tiles :]
    lam2 = jnp.concatenate([placed[8 * h : 8 * h + 8] for h in range(n_tiles)], axis=1)

    inverse = 0.1 / mass_ref[...]
    mu2 = lam2 * inverse
    w1[:, pl.ds(own, nodes)] = mu2
    disp = disp_ref[...]
    w1[0:3, pl.ds(own, nodes)] = disp

    peers = sum(jnp.where(exists(step), 1, 0) for step in steps)
    pl.semaphore_wait(barrier, peers)
    start_all(w1, send1, recv1)

    for i in range(4, 7):
        loads[i].wait()
    corner = conn_ref[0:1, :]
    corner_high = corner >> 7
    live = iota((1, slots), 1) < live_ref[0]
    scale_high, scale_low = pieces(jnp.where(live, stiff_ref[...], 0.0))
    on_row = iota((2 * n_tiles, slots), 0) == corner_high
    weighted = jnp.concatenate(
        [
            jnp.where(on_row, scale_high, 0.0).astype(BF16),
            jnp.where(on_row, scale_low, 0.0).astype(BF16),
        ],
        axis=0,
    )
    low_hot = jnp.where(iota((LANES, slots), 0) == (corner & (LANES - 1)), 1.0, 0.0).astype(BF16)
    both = dot(weighted, low_hot, 1)
    st[1] = both[: 2 * n_tiles] + both[2 * n_tiles :]
    for which in range(2):

        @pl.when(exists(steps[which]))
        def _(which=which):
            copy_factors(which).start()

    for i in range(7, 10):
        loads[i].wait()

    lane = iota((8, LANES), 1)

    def shift_tiles(w, first, last, keep):
        def turned(t):
            x = w[:, t * LANES : (t + 1) * LANES]
            return [x] + [pltpu.roll(x, LANES - off, 1) for off in OFFSETS[1:]]

        now = turned(first)
        for t in range(first, last):
            after = turned(t + 1)
            full = jnp.concatenate(
                [now[0]]
                + [
                    jnp.where(lane < LANES - off, now[i], after[i])
                    for i, off in enumerate(OFFSETS)
                    if i > 0
                ],
                axis=0,
            )
            if keep:
                xf[:, t * LANES : (t + 1) * LANES] = full
            high = full.astype(BF16)
            xs[0:32, t * LANES : (t + 1) * LANES] = high
            xs[32:64, t * LANES : (t + 1) * LANES] = (full - high.astype(F32)).astype(BF16)
            now = after

    def operand(start, width):
        return jnp.concatenate(
            [
                xs[:, start : start + width],
                xs[:, start + nodes : start + nodes + width],
                xs[0:32, start : start + width],
                xs[0:32, start + nodes : start + nodes + width],
            ],
            axis=0,
        )

    matrix = expanded_matrix(base_ref[...])
    carry[...] = 2.0 * mu2
    carry[0:3, :] = 2.0 * disp - prev_ref[...] + load_ref[:, 0, :] * inverse
    first_own = own // LANES
    last_tile = own // LANES + 2 * n_tiles
    shift_tiles(w1, first_own, first_own + n_tiles - 1, False)

    wait_arrivals(w1, send1, recv1)
    shift_tiles(w1, 0, first_own, False)
    shift_tiles(w1, first_own + n_tiles - 1, last_tile, False)

    for which in range(2):

        @pl.when(exists(-steps[which]))
        def _(which=which):
            copy_factors(which).wait_recv()

    def lower(tile):
        return st[tile // n_tiles, tile % n_tiles : tile % n_tiles + 1, :]

    def upper(tile):
        row = n_tiles + tile % n_tiles
        return st[tile // n_tiles, row : row + 1, :]

    totals = [lower(n_tiles - 1)] + [
        lower(t + n_tiles) + upper(t) for t in range(2 * n_tiles)
    ]
    total = jnp.concatenate([jnp.broadcast_to(x, (8, LANES)) for x in totals], axis=1)
    width = nodes + LANES

    def spread_sum(half0, half1):
        near, far = total[:, nodes:], total[:, :width]
        out = None
        for i, off in enumerate(OFFSETS):
            part = half0[8 * i : 8 * i + 8] * near + half1[8 * i : 8 * i + 8] * far
            part = pltpu.roll(part, off, 1) if off else part
            out = part if out is None else out + part
        return out[:, LANES:]

    p1[...] = dot(matrix, operand(0, cells))
    force = spread_sum(p1[0:32, nodes:], p1[32:64, :width])
    stepped = carry[...] - inverse * force
    w2[:, pl.ds(own, nodes)] = pltpu.roll(stepped, 4, 0)
    start_all(w2, send2, recv2)

    adjoint = pltpu.roll(3.0 * lam2 - 2.0 * force, 4, 0)
    carry[...] = 2.0 * stepped
    carry[0:3, :] = 2.0 * stepped[0:3] - disp + load_ref[:, 1, :] * inverse

    shift_tiles(w2, first_own, first_own + n_tiles - 1, True)
    wait_arrivals(w2, send2, recv2)
    shift_tiles(w2, 0, first_own, True)
    shift_tiles(w2, first_own + n_tiles - 1, last_tile, True)

    force2 = spread_sum(
        dot(matrix[0:32], operand(nodes, width)), dot(matrix[32:64], operand(0, width))
    )
    adj_out[...] = (adjoint - force2)[0:3]
    final = carry[...] - inverse * pltpu.roll(force2, 4, 0)

    picked = dot(
        jnp.concatenate(pieces(tiles_of(final)), axis=1),
        jnp.concatenate([sensor_hot, sensor_hot], axis=0),
    )
    response = jnp.zeros((8, sensors), F32)
    for h in range(n_tiles):
        response = response + jnp.where(sensor_high == h, picked[8 * h : 8 * h + 8], 0.0)
    resp_out[...] = response[0:3]

    energy = None
    for k in range(8):
        shift = LANES + (k // 4) * nodes
        part = (
            xf[8 * (k % 4) : 8 * (k % 4) + 8, shift : shift + 2 * nodes]
            * p1[8 * k : 8 * k + 8, LANES:cells]
        )
        energy = part if energy is None else energy + part
    tiles = [energy[:, t * LANES : (t + 1) * LANES] for t in range(2 * n_tiles)]
    sums = jnp.concatenate(
        [row_sums(tiles[t : t + 8]) for t in range(0, 2 * n_tiles, 8)], axis=0
    )
    table = jnp.concatenate(pieces(sums), axis=1)
    found = dot(table, jnp.concatenate([low_hot, low_hot], axis=0))
    gathered = jnp.sum(jnp.where(on_row, found, 0.0), axis=0, keepdims=True)
    sens_out[...] = jnp.where(live, -gathered, 0.0)

    for which in range(2):

        @pl.when(exists(steps[which]))
        def _(which=which):
            copy_factors(which).wait_send()

    wait_sent(w1, send1, recv1)
    wait_sent(w2, send2, recv2)


def store_kernel(sens, adj, resp, sens_out, adj_out, resp_out, sem):
    copies = [
        pltpu.make_async_copy(source, target, sem.at[i])
        for i, (source, target) in enumerate(((sens, sens_out), (adj, adj_out), (resp, resp_out)))
    ]
    for one in copies:
        one.start()
    for one in copies:
        one.wait()


def per_device(
    displacement,
    previous,
    traffic_load,
    lumped_mass,
    stiffness,
    base_matrix,
    connectivity,
    live_elements,
    sensor_nodes,
    sensor_weights,
):
    nodes = displacement.shape[1]
    slots = connectivity.shape[1]
    sensors = sensor_nodes.shape[0]
    count = lax.axis_size(CHAIN)
    window = 3 * nodes + 2 * LANES
    vmem = pl.BlockSpec(memory_space=pltpu.VMEM)
    hbm = pl.BlockSpec(memory_space=pltpu.HBM)
    operands = (
        displacement,
        previous,
        jnp.transpose(traffic_load, (1, 0, 2)),
        lumped_mass.reshape(1, nodes),
        stiffness.reshape(1, slots),
        base_matrix,
        connectivity,
        live_elements,
        sensor_nodes.reshape(1, sensors),
        sensor_weights,
    )
    results = pl.pallas_call(
        functools.partial(kernel, count),
        out_shape=(
            pltpu.VMEM((1, slots), F32),
            pltpu.VMEM((3, nodes), F32),
            pltpu.VMEM((3, sensors), F32),
        ),
        in_specs=[hbm] * len(operands),
        out_specs=(vmem, vmem, vmem),
        scratch_shapes=[
            (pltpu.SMEM if x is live_elements else pltpu.VMEM)(x.shape, x.dtype) for x in operands
        ]
        + [
            pltpu.SemaphoreType.DMA((len(operands),)),
            pltpu.VMEM((8, window), F32),
            pltpu.VMEM((8, window), F32),
            pltpu.VMEM((3, 2 * nodes // LANES, LANES), F32),
            pltpu.VMEM((64, window), BF16),
            pltpu.VMEM((32, window), F32),
            pltpu.VMEM((64, 2 * nodes + LANES), F32),
            pltpu.VMEM((8, nodes), F32),
            pltpu.VMEM((8, sensors), F32),
            pltpu.SemaphoreType.DMA((4,)),
            pltpu.SemaphoreType.DMA((4,)),
            pltpu.SemaphoreType.DMA((4,)),
            pltpu.SemaphoreType.DMA((4,)),
            pltpu.SemaphoreType.DMA((2,)),
            pltpu.SemaphoreType.DMA((2,)),
        ],
        compiler_params=pltpu.CompilerParams(
            collective_id=0, has_side_effects=True, vmem_limit_bytes=60 * 1024 * 1024
        ),
    )(*operands)
    sensitivity, adjoint_start, sensor_response = pl.pallas_call(
        store_kernel,
        out_shape=tuple(jax.ShapeDtypeStruct(x.shape, x.dtype) for x in results),
        in_specs=[vmem] * 3,
        out_specs=(hbm,) * 3,
        scratch_shapes=[pltpu.SemaphoreType.DMA((3,))],
        compiler_params=pltpu.CompilerParams(vmem_limit_bytes=4 * 1024 * 1024),
    )(*results)
    return sensitivity.reshape(slots), adjoint_start, sensor_response


def solution(mesh):
    in_specs = (
        P(None, ("event", "dom", "sub", "lane")),
        P(None, ("event", "dom", "sub", "lane")),
        P(None, None, ("event", "dom", "sub", "lane")),
        P(("dom", "sub", "lane")),
        P(("dom", "sub", "lane")),
        P(),
        P(None, ("dom", "sub", "lane")),
        P(("dom", "sub", "lane")),
        P(("dom", "sub", "lane")),
        P(None, ("event", "dom", "sub", "lane")),
    )
    out_specs = (
        P(("event", "dom", "sub", "lane")),
        P(None, ("event", "dom", "sub", "lane")),
        P(None, ("event", "dom", "sub", "lane")),
    )
    return jax.shard_map(
        per_device, mesh=mesh, in_specs=in_specs, out_specs=out_specs, check_vma=False
    )
```

```python
import functools

import jax
import jax.numpy as jnp
from jax import lax
from jax.experimental import pallas as pl
from jax.experimental.pallas import tpu as pltpu
from jax.sharding import PartitionSpec as P

F32 = jnp.float32
BF16 = jnp.bfloat16
I32 = jnp.int32
LANES = 128
OFFSETS = (0, 1, 4, 5)
CHAIN = ("dom", "sub", "lane")


def pieces(x):
    high = x.astype(BF16).astype(F32)
    return high, (x - high).astype(BF16).astype(F32)


def dot(a, b, rhs_dim=0):
    return lax.dot_general(
        a.astype(BF16), b.astype(BF16), (((1,), (rhs_dim,)), ((), ())), preferred_element_type=F32
    )


def iota(shape, dim):
    return lax.broadcasted_iota(I32, shape, dim)


def expanded_matrix(base):
    base_high, base_low = pieces(base)
    row = iota((64, 24), 0)
    comp = row & 3
    pick = jnp.where((iota((64, 24), 1) == comp * 8 + (row >> 3)) & (comp < 3), 1.0, 0.0)
    column = iota((24, 192), 1)
    group = column >> 5
    half = jnp.where(group < 4, group >> 1, group - 4)
    column_comp = column & 3
    node = half * 4 + ((column >> 3) & 3)
    spread = jnp.where((iota((24, 192), 0) == column_comp * 8 + node) & (column_comp < 3), 1.0, 0.0)
    high = dot(dot(pick, base_high), spread)
    low = dot(dot(pick, base_low), spread)
    out_row = iota((64, 192), 0)
    out_column = iota((64, 192), 1)
    same_field = ((out_row >> 2) & 1) == ((out_column >> 2) & 1)
    return jnp.where(same_field, jnp.where(out_column < 128, high, low), 0.0).astype(BF16)


def tiles_of(x):
    return jnp.concatenate(
        [x[:, s : s + LANES] for s in range(0, x.shape[1], LANES)], axis=0
    )


def row_sums(blocks):
    sub = iota((8, LANES), 0)
    step = 4
    while step:
        keep = (sub & step) == 0
        blocks = [
            jnp.where(keep, a, b)
            + jnp.where(keep, pltpu.roll(a, 8 - step, 0), pltpu.roll(b, step, 0))
            for a, b in zip(blocks[:step], blocks[step:])
        ]
        step //= 2
    return blocks[0]


def kernel(
    count,
    disp_hbm,
    prev_hbm,
    load_hbm,
    mass_hbm,
    stiff_hbm,
    base_hbm,
    conn_hbm,
    live_hbm,
    snode_hbm,
    sweight_hbm,
    sens_out,
    adj_out,
    resp_out,
    disp_ref,
    prev_ref,
    load_ref,
    mass_ref,
    stiff_ref,
    base_ref,
    conn_ref,
    live_ref,
    snode_ref,
    sweight_ref,
    loaded,
    w1,
    w2,
    st,
    xs,
    xf,
    p1,
    carry,
    w8,
    send1,
    recv1,
    send2,
    recv2,
    send3,
    recv3,
):
    nodes = disp_ref.shape[1]
    slots = stiff_ref.shape[1]
    sensors = snode_ref.shape[1]
    n_tiles = nodes // LANES
    own = LANES + nodes
    cells = 2 * nodes + LANES
    lanes_n = lax.axis_size("lane")
    subs_n = lax.axis_size("sub")
    me = (lax.axis_index("dom") * subs_n + lax.axis_index("sub")) * lanes_n + lax.axis_index("lane")

    def there(step):
        other = me + step
        return {
            "dom": lax.div(other, lanes_n * subs_n),
            "sub": lax.rem(lax.div(other, lanes_n), subs_n),
            "lane": lax.rem(other, lanes_n),
        }

    def exists(step):
        return (me + step < count) if step > 0 else (me + step >= 0)

    steps = (1, -1, 2, -2)
    barrier = pltpu.get_barrier_semaphore()
    for step in steps:

        @pl.when(exists(step))
        def _(step=step):
            pl.semaphore_signal(
                barrier, inc=1, device_id=there(step), device_id_type=pl.DeviceIdType.MESH
            )

    loads = {
        i: pltpu.make_async_copy(source, target, loaded.at[i])
        for i, (source, target) in enumerate(
            (
                (snode_hbm, snode_ref),
                (sweight_hbm, sweight_ref),
                (mass_hbm, mass_ref),
                (disp_hbm, disp_ref),
                (conn_hbm, conn_ref),
                (stiff_hbm, stiff_ref),
                (live_hbm, live_ref),
                (base_hbm, base_ref),
                (prev_hbm, prev_ref),
                (load_hbm, load_ref),
            )
        )
    }
    for load in loads.values():
        load.start()

    sources = {1: (own, nodes), -1: (own, nodes), 2: (own + nodes - LANES, LANES), -2: (own, LANES)}
    targets = {1: LANES, -1: own + nodes, 2: 0, -2: own + 2 * nodes}

    mid = n_tiles // 2
    own_tile = 1 + n_tiles
    first_tile = {1: 1, -1: 1 + 2 * n_tiles, 2: 1 - n_tiles, -2: 1 + 3 * n_tiles}
    parts1 = (
        (1, 0, mid + 2),
        (-1, 0, mid + 2),
        (1, mid + 2, n_tiles - mid - 2),
        (-1, mid + 2, n_tiles - mid - 2),
        (2, n_tiles - 1, 1),
        (-2, 0, 1),
    )
    parts2 = (
        (1, 1, mid),
        (-1, 1, mid),
        (1, mid + 1, n_tiles - mid - 1),
        (-1, mid + 1, n_tiles - mid - 1),
        (1, 0, 1),
        (-1, 0, 1),
        (2, n_tiles - 1, 1),
        (-2, 0, 1),
    )
    exchange1 = (w1, send1, recv1, parts1)
    exchange2 = (w2, send2, recv2, parts2)

    def copy(exchange, which):
        w, send, recv, parts = exchange
        step, first, tiles = parts[which]
        return pltpu.make_async_remote_copy(
            src_ref=w.at[:, pl.ds((own_tile + first) * LANES, tiles * LANES)],
            dst_ref=w.at[:, pl.ds((first_tile[step] + first) * LANES, tiles * LANES)],
            send_sem=send.at[which],
            recv_sem=recv.at[which],
            device_id=there(step),
            device_id_type=pl.DeviceIdType.MESH,
        )

    def start(exchange, first, last):
        for which in range(first, last):

            @pl.when(exists(exchange[3][which][0]))
            def _(which=which):
                copy(exchange, which).start()

    def wait_arrivals(exchange, first, last):
        for which in range(first, last):

            @pl.when(exists(-exchange[3][which][0]))
            def _(which=which):
                copy(exchange, which).wait_recv()

    def wait_sent(exchange):
        for which in range(len(exchange[3])):

            @pl.when(exists(exchange[3][which][0]))
            def _(which=which):
                copy(exchange, which).wait_send()

    for which, step in enumerate(steps):

        @pl.when(jnp.logical_not(exists(-step)))
        def _(step=step):
            width = sources[step][1]
            zero = jnp.zeros((8, width), F32)
            w1[:, pl.ds(targets[step], width)] = zero
            w2[:, pl.ds(targets[step], width)] = zero

    def copy_factors(which):
        return pltpu.make_async_remote_copy(
            src_ref=st.at[1],
            dst_ref=st.at[0 if which == 0 else 2],
            send_sem=send3.at[which],
            recv_sem=recv3.at[which],
            device_id=there(steps[which]),
            device_id_type=pl.DeviceIdType.MESH,
        )

    for which in range(2):

        @pl.when(jnp.logical_not(exists(-steps[which])))
        def _(which=which):
            st[0 if which == 0 else 2] = jnp.zeros((2 * n_tiles, LANES), F32)

    w8[...] = jnp.zeros((8, sensors), F32)
    for i in range(4):
        loads[i].wait()
    snode = snode_ref[...]
    sensor_high = snode >> 7
    sensor_hot = jnp.where(iota((LANES, sensors), 0) == (snode & (LANES - 1)), 1.0, 0.0).astype(BF16)
    w8[4:7, :] = sweight_ref[...]
    weight_high, weight_low = pieces(w8[...])
    stacked = jnp.concatenate(
        [
            jnp.where(sensor_high == h, part, 0.0)
            for part in (weight_high, weight_low)
            for h in range(n_tiles)
        ],
        axis=0,
    )
    placed = dot(stacked, sensor_hot, 1)
    placed = placed[: 8 * n_tiles] + placed[8 * n_tiles :]
    lam2 = jnp.concatenate([placed[8 * h : 8 * h + 8] for h in range(n_tiles)], axis=1)

    inverse = 0.1 / mass_ref[...]
    mu2 = lam2 * inverse
    w1[:, pl.ds(own, nodes)] = mu2
    disp = disp_ref[...]
    w1[0:3, pl.ds(own, nodes)] = disp

    peers = sum(jnp.where(exists(step), 1, 0) for step in steps)
    pl.semaphore_wait(barrier, peers)
    start(exchange1, 0, 6)

    for i in range(4, 7):
        loads[i].wait()
    corner = conn_ref[0:1, :]
    corner_high = corner >> 7
    live = iota((1, slots), 1) < live_ref[0]
    scale_high, scale_low = pieces(jnp.where(live, stiff_ref[...], 0.0))
    on_row = iota((2 * n_tiles, slots), 0) == corner_high
    weighted = jnp.concatenate(
        [
            jnp.where(on_row, scale_high, 0.0).astype(BF16),
            jnp.where(on_row, scale_low, 0.0).astype(BF16),
        ],
        axis=0,
    )
    low_hot = jnp.where(iota((LANES, slots), 0) == (corner & (LANES - 1)), 1.0, 0.0).astype(BF16)
    both = dot(weighted, low_hot, 1)
    st[1] = both[: 2 * n_tiles] + both[2 * n_tiles :]
    for which in range(2):

        @pl.when(exists(steps[which]))
        def _(which=which):
            copy_factors(which).start()

    for i in range(7, 10):
        loads[i].wait()

    lane = iota((8, LANES), 1)

    def shift_tiles(w, first, last, keep):
        def turned(t):
            x = w[:, t * LANES : (t + 1) * LANES]
            return [x] + [pltpu.roll(x, LANES - off, 1) for off in OFFSETS[1:]]

        now = turned(first)
        for t in range(first, last):
            after = turned(t + 1)
            full = jnp.concatenate(
                [now[0]]
                + [
                    jnp.where(lane < LANES - off, now[i], after[i])
                    for i, off in enumerate(OFFSETS)
                    if i > 0
                ],
                axis=0,
            )
            if keep:
                xf[:, t * LANES : (t + 1) * LANES] = full
            high = full.astype(BF16)
            xs[0:32, t * LANES : (t + 1) * LANES] = high
            xs[32:64, t * LANES : (t + 1) * LANES] = (full - high.astype(F32)).astype(BF16)
            now = after

    def operand(start, width):
        return jnp.concatenate(
            [
                xs[:, start : start + width],
                xs[:, start + nodes : start + nodes + width],
                xs[0:32, start : start + width],
                xs[0:32, start + nodes : start + nodes + width],
            ],
            axis=0,
        )

    matrix = expanded_matrix(base_ref[...])
    carry[...] = 2.0 * mu2
    carry[0:3, :] = 2.0 * disp - prev_ref[...] + load_ref[:, 0, :] * inverse
    last_tile = own_tile + 2 * n_tiles
    shift_tiles(w1, own_tile, own_tile + n_tiles - 1, False)
    wait_arrivals(exchange1, 0, 2)
    shift_tiles(w1, 1, mid + 2, False)
    shift_tiles(w1, own_tile + n_tiles, own_tile + n_tiles + mid + 1, False)

    for which in range(2):

        @pl.when(exists(-steps[which]))
        def _(which=which):
            copy_factors(which).wait_recv()

    def lower(tile):
        return st[tile // n_tiles, tile % n_tiles : tile % n_tiles + 1, :]

    def upper(tile):
        row = n_tiles + tile % n_tiles
        return st[tile // n_tiles, row : row + 1, :]

    totals = [lower(n_tiles - 1)] + [
        lower(t + n_tiles) + upper(t) for t in range(2 * n_tiles)
    ]
    totals = [jnp.broadcast_to(x, (8, LANES)) for x in totals]

    def spread_sum(first, last, half0, half1):
        near = jnp.concatenate(totals[first + n_tiles : last + n_tiles + 1], axis=1)
        far = jnp.concatenate(totals[first : last + 1], axis=1)
        out = None
        for i, off in enumerate(OFFSETS):
            part = half0[8 * i : 8 * i + 8] * near + half1[8 * i : 8 * i + 8] * far
            part = pltpu.roll(part, off, 1) if off else part
            out = part if out is None else out + part
        return out[:, LANES:]

    def multiply(first, last):
        p1[:, first * LANES : last * LANES] = dot(
            matrix, operand(first * LANES, (last - first) * LANES)
        )

    def step_one(first, last):
        force = spread_sum(
            first,
            last,
            p1[0:32, (first + n_tiles) * LANES : (last + n_tiles + 1) * LANES],
            p1[32:64, first * LANES : (last + 1) * LANES],
        )
        here = slice(first * LANES, last * LANES)
        stepped = carry[:, here] - inverse[:, here] * force
        w2[:, (own_tile + first) * LANES : (own_tile + last) * LANES] = pltpu.roll(stepped, 4, 0)
        return force, stepped

    multiply(1, mid + 2)
    multiply(own_tile, own_tile + mid + 1)
    force_a, stepped_a = step_one(1, mid + 1)
    start(exchange2, 0, 2)

    wait_arrivals(exchange1, 2, 6)
    shift_tiles(w1, 0, 1, False)
    shift_tiles(w1, mid + 2, own_tile, False)
    shift_tiles(w1, own_tile + n_tiles - 1, own_tile + n_tiles, False)
    shift_tiles(w1, own_tile + n_tiles + mid + 1, last_tile, False)
    multiply(0, 1)
    multiply(mid + 2, own_tile)
    multiply(own_tile + mid + 1, 1 + 2 * n_tiles)
    force_0, stepped_0 = step_one(0, 1)
    force_b, stepped_b = step_one(mid + 1, n_tiles)
    start(exchange2, 2, 8)
    force = jnp.concatenate([force_0, force_a, force_b], axis=1)
    stepped = jnp.concatenate([stepped_0, stepped_a, stepped_b], axis=1)

    adjoint = pltpu.roll(3.0 * lam2 - 2.0 * force, 4, 0)
    carry[...] = 2.0 * stepped
    carry[0:3, :] = 2.0 * stepped[0:3] - disp + load_ref[:, 1, :] * inverse

    shift_tiles(w2, own_tile, own_tile + n_tiles - 1, True)
    wait_arrivals(exchange2, 0, 2)
    shift_tiles(w2, 2, mid + 1, True)
    shift_tiles(w2, own_tile + n_tiles + 1, own_tile + n_tiles + mid, True)
    wait_arrivals(exchange2, 2, 8)
    shift_tiles(w2, 0, 2, True)
    shift_tiles(w2, mid + 1, own_tile, True)
    shift_tiles(w2, own_tile + n_tiles - 1, own_tile + n_tiles + 1, True)
    shift_tiles(w2, own_tile + n_tiles + mid, last_tile, True)

    width = nodes + LANES
    force2 = spread_sum(
        0, n_tiles, dot(matrix[0:32], operand(nodes, width)), dot(matrix[32:64], operand(0, width))
    )
    adj_out[...] = (adjoint - force2)[0:3]
    final = carry[...] - inverse * pltpu.roll(force2, 4, 0)

    picked = dot(
        jnp.concatenate(pieces(tiles_of(final)), axis=1),
        jnp.concatenate([sensor_hot, sensor_hot], axis=0),
    )
    response = jnp.zeros((8, sensors), F32)
    for h in range(n_tiles):
        response = response + jnp.where(sensor_high == h, picked[8 * h : 8 * h + 8], 0.0)
    resp_out[...] = response[0:3]

    energy = None
    for k in range(8):
        shift = LANES + (k // 4) * nodes
        part = (
            xf[8 * (k % 4) : 8 * (k % 4) + 8, shift : shift + 2 * nodes]
            * p1[8 * k : 8 * k + 8, LANES:cells]
        )
        energy = part if energy is None else energy + part
    tiles = [energy[:, t * LANES : (t + 1) * LANES] for t in range(2 * n_tiles)]
    sums = jnp.concatenate(
        [row_sums(tiles[t : t + 8]) for t in range(0, 2 * n_tiles, 8)], axis=0
    )
    table = jnp.concatenate(pieces(sums), axis=1)
    found = dot(table, jnp.concatenate([low_hot, low_hot], axis=0))
    gathered = jnp.sum(jnp.where(on_row, found, 0.0), axis=0, keepdims=True)
    sens_out[...] = jnp.where(live, -gathered, 0.0)

    for which in range(2):

        @pl.when(exists(steps[which]))
        def _(which=which):
            copy_factors(which).wait_send()

    wait_sent(exchange1)
    wait_sent(exchange2)


def store_kernel(sens, adj, resp, sens_out, adj_out, resp_out, sem):
    copies = [
        pltpu.make_async_copy(source, target, sem.at[i])
        for i, (source, target) in enumerate(((sens, sens_out), (adj, adj_out), (resp, resp_out)))
    ]
    for one in copies:
        one.start()
    for one in copies:
        one.wait()


def per_device(
    displacement,
    previous,
    traffic_load,
    lumped_mass,
    stiffness,
    base_matrix,
    connectivity,
    live_elements,
    sensor_nodes,
    sensor_weights,
):
    nodes = displacement.shape[1]
    slots = connectivity.shape[1]
    sensors = sensor_nodes.shape[0]
    count = lax.axis_size(CHAIN)
    window = 3 * nodes + 2 * LANES
    vmem = pl.BlockSpec(memory_space=pltpu.VMEM)
    hbm = pl.BlockSpec(memory_space=pltpu.HBM)
    operands = (
        displacement,
        previous,
        jnp.transpose(traffic_load, (1, 0, 2)),
        lumped_mass.reshape(1, nodes),
        stiffness.reshape(1, slots),
        base_matrix,
        connectivity,
        live_elements,
        sensor_nodes.reshape(1, sensors),
        sensor_weights,
    )
    results = pl.pallas_call(
        functools.partial(kernel, count),
        out_shape=(
            pltpu.VMEM((1, slots), F32),
            pltpu.VMEM((3, nodes), F32),
            pltpu.VMEM((3, sensors), F32),
        ),
        in_specs=[hbm] * len(operands),
        out_specs=(vmem, vmem, vmem),
        scratch_shapes=[
            (pltpu.SMEM if x is live_elements else pltpu.VMEM)(x.shape, x.dtype) for x in operands
        ]
        + [
            pltpu.SemaphoreType.DMA((len(operands),)),
            pltpu.VMEM((8, window), F32),
            pltpu.VMEM((8, window), F32),
            pltpu.VMEM((3, 2 * nodes // LANES, LANES), F32),
            pltpu.VMEM((64, window), BF16),
            pltpu.VMEM((32, window), F32),
            pltpu.VMEM((64, 2 * nodes + LANES), F32),
            pltpu.VMEM((8, nodes), F32),
            pltpu.VMEM((8, sensors), F32),
            pltpu.SemaphoreType.DMA((6,)),
            pltpu.SemaphoreType.DMA((6,)),
            pltpu.SemaphoreType.DMA((8,)),
            pltpu.SemaphoreType.DMA((8,)),
            pltpu.SemaphoreType.DMA((2,)),
            pltpu.SemaphoreType.DMA((2,)),
        ],
        compiler_params=pltpu.CompilerParams(
            collective_id=0, has_side_effects=True, vmem_limit_bytes=60 * 1024 * 1024
        ),
    )(*operands)
    sensitivity, adjoint_start, sensor_response = pl.pallas_call(
        store_kernel,
        out_shape=tuple(jax.ShapeDtypeStruct(x.shape, x.dtype) for x in results),
        in_specs=[vmem] * 3,
        out_specs=(hbm,) * 3,
        scratch_shapes=[pltpu.SemaphoreType.DMA((3,))],
        compiler_params=pltpu.CompilerParams(vmem_limit_bytes=4 * 1024 * 1024),
    )(*results)
    return sensitivity.reshape(slots), adjoint_start, sensor_response


def solution(mesh):
    in_specs = (
        P(None, ("event", "dom", "sub", "lane")),
        P(None, ("event", "dom", "sub", "lane")),
        P(None, None, ("event", "dom", "sub", "lane")),
        P(("dom", "sub", "lane")),
        P(("dom", "sub", "lane")),
        P(),
        P(None, ("dom", "sub", "lane")),
        P(("dom", "sub", "lane")),
        P(("dom", "sub", "lane")),
        P(None, ("event", "dom", "sub", "lane")),
    )
    out_specs = (
        P(("event", "dom", "sub", "lane")),
        P(None, ("event", "dom", "sub", "lane")),
        P(None, ("event", "dom", "sub", "lane")),
    )
    return jax.shard_map(
        per_device, mesh=mesh, in_specs=in_specs, out_specs=out_specs, check_vma=False
    )
```

```python
import functools

import jax
import jax.numpy as jnp
from jax import lax
from jax.experimental import pallas as pl
from jax.experimental.pallas import tpu as pltpu
from jax.sharding import PartitionSpec as P

F32 = jnp.float32
BF16 = jnp.bfloat16
I32 = jnp.int32
LANES = 128
OFFSETS = (0, 1, 4, 5)
CHAIN = ("dom", "sub", "lane")


def pieces(x):
    high = x.astype(BF16).astype(F32)
    return high, (x - high).astype(BF16).astype(F32)


def dot(a, b, rhs_dim=0):
    return lax.dot_general(
        a.astype(BF16), b.astype(BF16), (((1,), (rhs_dim,)), ((), ())), preferred_element_type=F32
    )


def iota(shape, dim):
    return lax.broadcasted_iota(I32, shape, dim)


def expanded_matrix(base):
    base_high, base_low = pieces(base)
    row = iota((64, 24), 0)
    comp = row & 3
    pick = jnp.where((iota((64, 24), 1) == comp * 8 + (row >> 3)) & (comp < 3), 1.0, 0.0)
    column = iota((24, 192), 1)
    group = column >> 5
    half = jnp.where(group < 4, group >> 1, group - 4)
    column_comp = column & 3
    node = half * 4 + ((column >> 3) & 3)
    spread = jnp.where((iota((24, 192), 0) == column_comp * 8 + node) & (column_comp < 3), 1.0, 0.0)
    high = dot(dot(pick, base_high), spread)
    low = dot(dot(pick, base_low), spread)
    out_row = iota((64, 192), 0)
    out_column = iota((64, 192), 1)
    same_field = ((out_row >> 2) & 1) == ((out_column >> 2) & 1)
    return jnp.where(same_field, jnp.where(out_column < 128, high, low), 0.0).astype(BF16)


def tiles_of(x):
    return jnp.concatenate(
        [x[:, s : s + LANES] for s in range(0, x.shape[1], LANES)], axis=0
    )


def row_sums(blocks):
    sub = iota((8, LANES), 0)
    step = 4
    while step:
        keep = (sub & step) == 0
        blocks = [
            jnp.where(keep, a, b)
            + jnp.where(keep, pltpu.roll(a, 8 - step, 0), pltpu.roll(b, step, 0))
            for a, b in zip(blocks[:step], blocks[step:])
        ]
        step //= 2
    return blocks[0]


def kernel(
    count,
    disp_hbm,
    prev_hbm,
    load_hbm,
    mass_hbm,
    stiff_hbm,
    base_hbm,
    conn_hbm,
    live_hbm,
    snode_hbm,
    sweight_hbm,
    sens_out,
    adj_out,
    resp_out,
    disp_ref,
    prev_ref,
    load_ref,
    mass_ref,
    stiff_ref,
    base_ref,
    conn_ref,
    live_ref,
    snode_ref,
    sweight_ref,
    loaded,
    w1,
    w2,
    st,
    xs,
    xf,
    p1,
    p2,
    carry,
    w8,
    send1,
    recv1,
    send2,
    recv2,
    send3,
    recv3,
):
    nodes = disp_ref.shape[1]
    slots = stiff_ref.shape[1]
    sensors = snode_ref.shape[1]
    n_tiles = nodes // LANES
    own = LANES + nodes
    cells = 2 * nodes + LANES
    lanes_n = lax.axis_size("lane")
    subs_n = lax.axis_size("sub")
    me = (lax.axis_index("dom") * subs_n + lax.axis_index("sub")) * lanes_n + lax.axis_index("lane")

    def there(step):
        other = me + step
        return {
            "dom": lax.div(other, lanes_n * subs_n),
            "sub": lax.rem(lax.div(other, lanes_n), subs_n),
            "lane": lax.rem(other, lanes_n),
        }

    def exists(step):
        return (me + step < count) if step > 0 else (me + step >= 0)

    steps = (1, -1, 2, -2)
    barrier = pltpu.get_barrier_semaphore()
    for step in steps:

        @pl.when(exists(step))
        def _(step=step):
            pl.semaphore_signal(
                barrier, inc=1, device_id=there(step), device_id_type=pl.DeviceIdType.MESH
            )

    loads = {
        i: pltpu.make_async_copy(source, target, loaded.at[i])
        for i, (source, target) in enumerate(
            (
                (snode_hbm, snode_ref),
                (sweight_hbm, sweight_ref),
                (mass_hbm, mass_ref),
                (disp_hbm, disp_ref),
                (conn_hbm, conn_ref),
                (stiff_hbm, stiff_ref),
                (live_hbm, live_ref),
                (base_hbm, base_ref),
                (prev_hbm, prev_ref),
                (load_hbm, load_ref),
            )
        )
    }
    for load in loads.values():
        load.start()

    sources = {1: (own, nodes), -1: (own, nodes), 2: (own + nodes - LANES, LANES), -2: (own, LANES)}
    targets = {1: LANES, -1: own + nodes, 2: 0, -2: own + 2 * nodes}

    mid = n_tiles // 2
    own_tile = 1 + n_tiles
    first_tile = {1: 1, -1: 1 + 2 * n_tiles, 2: 1 - n_tiles, -2: 1 + 3 * n_tiles}
    parts1 = (
        (1, 0, mid + 2),
        (-1, 0, mid + 2),
        (1, mid + 2, n_tiles - mid - 2),
        (-1, mid + 2, n_tiles - mid - 2),
        (2, n_tiles - 1, 1),
        (-2, 0, 1),
    )
    parts2 = (
        (1, 1, mid),
        (-1, 1, mid),
        (1, mid + 1, n_tiles - mid - 1),
        (-1, mid + 1, n_tiles - mid - 1),
        (1, 0, 1),
        (-1, 0, 1),
        (2, n_tiles - 1, 1),
        (-2, 0, 1),
    )
    exchange1 = (w1, send1, recv1, parts1)
    exchange2 = (w2, send2, recv2, parts2)

    def copy(exchange, which):
        w, send, recv, parts = exchange
        step, first, tiles = parts[which]
        return pltpu.make_async_remote_copy(
            src_ref=w.at[:, pl.ds((own_tile + first) * LANES, tiles * LANES)],
            dst_ref=w.at[:, pl.ds((first_tile[step] + first) * LANES, tiles * LANES)],
            send_sem=send.at[which],
            recv_sem=recv.at[which],
            device_id=there(step),
            device_id_type=pl.DeviceIdType.MESH,
        )

    def start(exchange, first, last):
        for which in range(first, last):

            @pl.when(exists(exchange[3][which][0]))
            def _(which=which):
                copy(exchange, which).start()

    def wait_arrivals(exchange, first, last):
        for which in range(first, last):

            @pl.when(exists(-exchange[3][which][0]))
            def _(which=which):
                copy(exchange, which).wait_recv()

    def wait_sent(exchange):
        for which in range(len(exchange[3])):

            @pl.when(exists(exchange[3][which][0]))
            def _(which=which):
                copy(exchange, which).wait_send()

    for which, step in enumerate(steps):

        @pl.when(jnp.logical_not(exists(-step)))
        def _(step=step):
            width = sources[step][1]
            zero = jnp.zeros((8, width), F32)
            w1[:, pl.ds(targets[step], width)] = zero
            w2[:, pl.ds(targets[step], width)] = zero

    def copy_factors(which):
        return pltpu.make_async_remote_copy(
            src_ref=st.at[1],
            dst_ref=st.at[0 if which == 0 else 2],
            send_sem=send3.at[which],
            recv_sem=recv3.at[which],
            device_id=there(steps[which]),
            device_id_type=pl.DeviceIdType.MESH,
        )

    for which in range(2):

        @pl.when(jnp.logical_not(exists(-steps[which])))
        def _(which=which):
            st[0 if which == 0 else 2] = jnp.zeros((2 * n_tiles, LANES), F32)

    w8[...] = jnp.zeros((8, sensors), F32)
    for i in range(4):
        loads[i].wait()
    snode = snode_ref[...]
    sensor_high = snode >> 7
    sensor_hot = jnp.where(iota((LANES, sensors), 0) == (snode & (LANES - 1)), 1.0, 0.0).astype(BF16)
    w8[4:7, :] = sweight_ref[...]
    weight_high, weight_low = pieces(w8[...])
    stacked = jnp.concatenate(
        [
            jnp.where(sensor_high == h, part, 0.0)
            for part in (weight_high, weight_low)
            for h in range(n_tiles)
        ],
        axis=0,
    )
    placed = dot(stacked, sensor_hot, 1)
    placed = placed[: 8 * n_tiles] + placed[8 * n_tiles :]
    lam2 = jnp.concatenate([placed[8 * h : 8 * h + 8] for h in range(n_tiles)], axis=1)

    inverse = 0.1 / mass_ref[...]
    mu2 = lam2 * inverse
    w1[:, pl.ds(own, nodes)] = mu2
    disp = disp_ref[...]
    w1[0:3, pl.ds(own, nodes)] = disp

    peers = sum(jnp.where(exists(step), 1, 0) for step in steps)
    pl.semaphore_wait(barrier, peers)
    start(exchange1, 0, 6)

    for i in range(4, 7):
        loads[i].wait()
    corner = conn_ref[0:1, :]
    corner_high = corner >> 7
    live = iota((1, slots), 1) < live_ref[0]
    scale_high, scale_low = pieces(jnp.where(live, stiff_ref[...], 0.0))
    on_row = iota((2 * n_tiles, slots), 0) == corner_high
    weighted = jnp.concatenate(
        [
            jnp.where(on_row, scale_high, 0.0).astype(BF16),
            jnp.where(on_row, scale_low, 0.0).astype(BF16),
        ],
        axis=0,
    )
    low_hot = jnp.where(iota((LANES, slots), 0) == (corner & (LANES - 1)), 1.0, 0.0).astype(BF16)
    both = dot(weighted, low_hot, 1)
    st[1] = both[: 2 * n_tiles] + both[2 * n_tiles :]
    for which in range(2):

        @pl.when(exists(steps[which]))
        def _(which=which):
            copy_factors(which).start()

    for i in range(7, 10):
        loads[i].wait()

    lane = iota((8, LANES), 1)

    def shift_tiles(w, first, last, keep):
        def turned(t):
            x = w[:, t * LANES : (t + 1) * LANES]
            return [x] + [pltpu.roll(x, LANES - off, 1) for off in OFFSETS[1:]]

        now = turned(first)
        for t in range(first, last):
            after = turned(t + 1)
            full = jnp.concatenate(
                [now[0]]
                + [
                    jnp.where(lane < LANES - off, now[i], after[i])
                    for i, off in enumerate(OFFSETS)
                    if i > 0
                ],
                axis=0,
            )
            if keep:
                xf[:, t * LANES : (t + 1) * LANES] = full
            high = full.astype(BF16)
            xs[0:32, t * LANES : (t + 1) * LANES] = high
            xs[32:64, t * LANES : (t + 1) * LANES] = (full - high.astype(F32)).astype(BF16)
            now = after

    def operand(start, width):
        return jnp.concatenate(
            [
                xs[:, start : start + width],
                xs[:, start + nodes : start + nodes + width],
                xs[0:32, start : start + width],
                xs[0:32, start + nodes : start + nodes + width],
            ],
            axis=0,
        )

    matrix = expanded_matrix(base_ref[...])
    carry[...] = 2.0 * mu2
    carry[0:3, :] = 2.0 * disp - prev_ref[...] + load_ref[:, 0, :] * inverse
    last_tile = own_tile + 2 * n_tiles
    shift_tiles(w1, own_tile, own_tile + n_tiles - 1, False)
    wait_arrivals(exchange1, 0, 2)
    shift_tiles(w1, 1, mid + 2, False)
    shift_tiles(w1, own_tile + n_tiles, own_tile + n_tiles + mid + 1, False)

    for which in range(2):

        @pl.when(exists(-steps[which]))
        def _(which=which):
            copy_factors(which).wait_recv()

    def lower(tile):
        return st[tile // n_tiles, tile % n_tiles : tile % n_tiles + 1, :]

    def upper(tile):
        row = n_tiles + tile % n_tiles
        return st[tile // n_tiles, row : row + 1, :]

    totals = [lower(n_tiles - 1)] + [
        lower(t + n_tiles) + upper(t) for t in range(2 * n_tiles)
    ]
    totals = [jnp.broadcast_to(x, (8, LANES)) for x in totals]

    def spread_sum(first, last, half0, half1):
        near = jnp.concatenate(totals[first + n_tiles : last + n_tiles + 1], axis=1)
        far = jnp.concatenate(totals[first : last + 1], axis=1)
        out = None
        for i, off in enumerate(OFFSETS):
            part = half0[8 * i : 8 * i + 8] * near + half1[8 * i : 8 * i + 8] * far
            part = pltpu.roll(part, off, 1) if off else part
            out = part if out is None else out + part
        return out[:, LANES:]

    def multiply(first, last):
        p1[:, first * LANES : last * LANES] = dot(
            matrix, operand(first * LANES, (last - first) * LANES)
        )

    def step_one(first, last):
        force = spread_sum(
            first,
            last,
            p1[0:32, (first + n_tiles) * LANES : (last + n_tiles + 1) * LANES],
            p1[32:64, first * LANES : (last + 1) * LANES],
        )
        here = slice(first * LANES, last * LANES)
        stepped = carry[:, here] - inverse[:, here] * force
        w2[:, (own_tile + first) * LANES : (own_tile + last) * LANES] = pltpu.roll(stepped, 4, 0)
        return force, stepped

    multiply(1, mid + 2)
    multiply(own_tile, own_tile + mid + 1)
    force_a, stepped_a = step_one(1, mid + 1)
    start(exchange2, 0, 2)

    wait_arrivals(exchange1, 2, 6)
    shift_tiles(w1, 0, 1, False)
    shift_tiles(w1, mid + 2, own_tile, False)
    shift_tiles(w1, own_tile + n_tiles - 1, own_tile + n_tiles, False)
    shift_tiles(w1, own_tile + n_tiles + mid + 1, last_tile, False)
    multiply(0, 1)
    multiply(mid + 2, own_tile)
    multiply(own_tile + mid + 1, 1 + 2 * n_tiles)
    force_0, stepped_0 = step_one(0, 1)
    force_b, stepped_b = step_one(mid + 1, n_tiles)
    start(exchange2, 2, 8)
    force = jnp.concatenate([force_0, force_a, force_b], axis=1)
    stepped = jnp.concatenate([stepped_0, stepped_a, stepped_b], axis=1)

    adjoint = pltpu.roll(3.0 * lam2 - 2.0 * force, 4, 0)
    carry[...] = 2.0 * stepped
    carry[0:3, :] = 2.0 * stepped[0:3] - disp + load_ref[:, 1, :] * inverse

    def multiply_two(first, last):
        width = (last - first) * LANES
        here = slice(first * LANES, last * LANES)
        p2[0:32, here] = dot(matrix[0:32], operand(first * LANES + nodes, width))
        p2[32:64, here] = dot(matrix[32:64], operand(first * LANES, width))

    def energy_of(first, last):
        found = {}
        for t in range(first, last):
            value = None
            for k in range(8):
                at = (t + (k // 4) * n_tiles) * LANES
                part = (
                    xf[8 * (k % 4) : 8 * (k % 4) + 8, at : at + LANES]
                    * p1[8 * k : 8 * k + 8, t * LANES : (t + 1) * LANES]
                )
                value = part if value is None else value + part
            found[t] = value
        return found

    shift_tiles(w2, own_tile, own_tile + n_tiles - 1, True)
    wait_arrivals(exchange2, 0, 2)
    shift_tiles(w2, 2, mid + 1, True)
    shift_tiles(w2, own_tile + n_tiles + 1, own_tile + n_tiles + mid, True)
    multiply_two(2, mid + 1)
    energy = energy_of(2, mid + 1) | energy_of(own_tile + 1, own_tile + mid)
    wait_arrivals(exchange2, 2, 8)
    shift_tiles(w2, 0, 2, True)
    shift_tiles(w2, mid + 1, own_tile, True)
    shift_tiles(w2, own_tile + n_tiles - 1, own_tile + n_tiles + 1, True)
    shift_tiles(w2, own_tile + n_tiles + mid, last_tile, True)

    multiply_two(0, 2)
    multiply_two(mid + 1, n_tiles + 1)
    force2 = spread_sum(0, n_tiles, p2[0:32, :], p2[32:64, :])
    adj_out[...] = (adjoint - force2)[0:3]
    final = carry[...] - inverse * pltpu.roll(force2, 4, 0)

    picked = dot(
        jnp.concatenate(pieces(tiles_of(final)), axis=1),
        jnp.concatenate([sensor_hot, sensor_hot], axis=0),
    )
    response = jnp.zeros((8, sensors), F32)
    for h in range(n_tiles):
        response = response + jnp.where(sensor_high == h, picked[8 * h : 8 * h + 8], 0.0)
    resp_out[...] = response[0:3]

    energy |= energy_of(1, 2) | energy_of(mid + 1, own_tile + 1)
    energy |= energy_of(own_tile + mid, own_tile + n_tiles)
    tiles = [energy[t + 1] for t in range(2 * n_tiles)]
    sums = jnp.concatenate(
        [row_sums(tiles[t : t + 8]) for t in range(0, 2 * n_tiles, 8)], axis=0
    )
    table = jnp.concatenate(pieces(sums), axis=1)
    found = dot(table, jnp.concatenate([low_hot, low_hot], axis=0))
    gathered = jnp.sum(jnp.where(on_row, found, 0.0), axis=0, keepdims=True)
    sens_out[...] = jnp.where(live, -gathered, 0.0)

    for which in range(2):

        @pl.when(exists(steps[which]))
        def _(which=which):
            copy_factors(which).wait_send()

    wait_sent(exchange1)
    wait_sent(exchange2)


def store_kernel(sens, adj, resp, sens_out, adj_out, resp_out, sem):
    copies = [
        pltpu.make_async_copy(source, target, sem.at[i])
        for i, (source, target) in enumerate(((sens, sens_out), (adj, adj_out), (resp, resp_out)))
    ]
    for one in copies:
        one.start()
    for one in copies:
        one.wait()


def per_device(
    displacement,
    previous,
    traffic_load,
    lumped_mass,
    stiffness,
    base_matrix,
    connectivity,
    live_elements,
    sensor_nodes,
    sensor_weights,
):
    nodes = displacement.shape[1]
    slots = connectivity.shape[1]
    sensors = sensor_nodes.shape[0]
    count = lax.axis_size(CHAIN)
    window = 3 * nodes + 2 * LANES
    vmem = pl.BlockSpec(memory_space=pltpu.VMEM)
    hbm = pl.BlockSpec(memory_space=pltpu.HBM)
    operands = (
        displacement,
        previous,
        jnp.transpose(traffic_load, (1, 0, 2)),
        lumped_mass.reshape(1, nodes),
        stiffness.reshape(1, slots),
        base_matrix,
        connectivity,
        live_elements,
        sensor_nodes.reshape(1, sensors),
        sensor_weights,
    )
    results = pl.pallas_call(
        functools.partial(kernel, count),
        out_shape=(
            pltpu.VMEM((1, slots), F32),
            pltpu.VMEM((3, nodes), F32),
            pltpu.VMEM((3, sensors), F32),
        ),
        in_specs=[hbm] * len(operands),
        out_specs=(vmem, vmem, vmem),
        scratch_shapes=[
            (pltpu.SMEM if x is live_elements else pltpu.VMEM)(x.shape, x.dtype) for x in operands
        ]
        + [
            pltpu.SemaphoreType.DMA((len(operands),)),
            pltpu.VMEM((8, window), F32),
            pltpu.VMEM((8, window), F32),
            pltpu.VMEM((3, 2 * nodes // LANES, LANES), F32),
            pltpu.VMEM((64, window), BF16),
            pltpu.VMEM((32, window), F32),
            pltpu.VMEM((64, 2 * nodes + LANES), F32),
            pltpu.VMEM((64, nodes + LANES), F32),
            pltpu.VMEM((8, nodes), F32),
            pltpu.VMEM((8, sensors), F32),
            pltpu.SemaphoreType.DMA((6,)),
            pltpu.SemaphoreType.DMA((6,)),
            pltpu.SemaphoreType.DMA((8,)),
            pltpu.SemaphoreType.DMA((8,)),
            pltpu.SemaphoreType.DMA((2,)),
            pltpu.SemaphoreType.DMA((2,)),
        ],
        compiler_params=pltpu.CompilerParams(
            collective_id=0, has_side_effects=True, vmem_limit_bytes=60 * 1024 * 1024
        ),
    )(*operands)
    sensitivity, adjoint_start, sensor_response = pl.pallas_call(
        store_kernel,
        out_shape=tuple(jax.ShapeDtypeStruct(x.shape, x.dtype) for x in results),
        in_specs=[vmem] * 3,
        out_specs=(hbm,) * 3,
        scratch_shapes=[pltpu.SemaphoreType.DMA((3,))],
        compiler_params=pltpu.CompilerParams(vmem_limit_bytes=4 * 1024 * 1024),
    )(*results)
    return sensitivity.reshape(slots), adjoint_start, sensor_response


def solution(mesh):
    in_specs = (
        P(None, ("event", "dom", "sub", "lane")),
        P(None, ("event", "dom", "sub", "lane")),
        P(None, None, ("event", "dom", "sub", "lane")),
        P(("dom", "sub", "lane")),
        P(("dom", "sub", "lane")),
        P(),
        P(None, ("dom", "sub", "lane")),
        P(("dom", "sub", "lane")),
        P(("dom", "sub", "lane")),
        P(None, ("event", "dom", "sub", "lane")),
    )
    out_specs = (
        P(("event", "dom", "sub", "lane")),
        P(None, ("event", "dom", "sub", "lane")),
        P(None, ("event", "dom", "sub", "lane")),
    )
    return jax.shard_map(
        per_device, mesh=mesh, in_specs=in_specs, out_specs=out_specs, check_vma=False
    )
```
